512 devices in a mesh: dp: 16 (over z), expert: 32 (over y, x, core).
Axes of the slice: x: 4, y: 4, z: 16, core: 2. Of those that a mesh axis runs over, the one named last changes fastest.
Arguments:
- train_x: bfloat16 [65536, 5120], P(('dp', 'expert')), may hold values from -6 to 6
- train_grad: bfloat16 [65536, 6, 1536], P(('dp', 'expert')), may hold values from -0.119628906 to 0.119628906
- train_routes: int32 [65536, 6], P(('dp', 'expert')), may hold values from 0 to 159, all different within a row; in each aligned block of 128 rows (0 to 127, 128 to 255, ...) at most 6 rows name the same one
- train_weight: float32 [65536, 6], P(('dp', 'expert')), may hold values from 0.05 to 1
- train_example: int32 [65536], P(('dp', 'expert')), may hold values from 0 to 3
- probe_x: bfloat16 [1024, 5120], P('dp'), may hold values from -6 to 6
- probe_grad: bfloat16 [1024, 6, 1536], P('dp'), may hold values from -0.119628906 to 0.119628906
- probe_routes: int32 [1024, 6], P('dp'), may hold values from 0 to 159, all different within a row; in each aligned block of 64 rows (0 to 63, 64 to 127, ...) at most 3 rows name the same one
- probe_weight: float32 [1024, 6], P('dp'), may hold values from 0.05 to 1
- probe_example: int32 [1024], P('dp'), may hold values from 0 to 7
Outputs:
- scores: float32 [2048, 128], P(('dp', 'expert'))
The draws below stay inside these ranges and needn't reach their ends.
Inputs may be any that keep to these rules, and one draw needn't show every extreme that they name: `train_routes`: in the rows of one device no expert is named more than 6 times, a bound that some block reaches. `probe_routes`: in the rows of one index of dp no expert is named more than 3 times, a bound that some block reaches.
All inputs are finite; a program needn't handle non-finite values.
Results may differ from the reference program's by a relative error of at most 0.004.
Values may be sent and summed in bfloat16 or wider, within the bound.
A program may use at most 128 MiB of HBM per device.

```python
import math
from functools import partial
import jax
import jax.numpy as jnp
import numpy as np
from jax import lax

D = 5120
FF = 1536
TOP = 6
TOK_DEV = 128
P_ROW = 64
EX_DEV = 4
PEX_ROW = 8
EXPERTS = 160
CAP = 6
PCAP = 3
TRAIN = 65536
PROBE = 1024
TRAIN_EX = 2048
PROBE_EX = 128
N_DP = 16
N_EXPERT = 32


def set_ends(values, rng, smallest, top_value):
    shape = values.shape
    place = [jax.random.randint(jax.random.fold_in(rng, axis), (), 0, shape[axis]) for axis in range(len(shape))]
    values = values.at[tuple(place)].set(smallest)
    longest = shape.index(max(shape))
    place[longest] = (place[longest] + 1) % shape[longest]
    return values.at[tuple(place)].set(top_value)


def block_scale(key, extent, split, low, high):
    loudness = 1.0
    for position, parts in split:
        steps = jax.random.uniform(jax.random.fold_in(jax.random.fold_in(key, 6), position), (parts,), jnp.float32, low / len(split), high / len(split))
        loudness = loudness * jnp.repeat(jnp.exp(steps), extent[position] // parts).reshape((-1,) + (1,) * (len(extent) - 1 - position))
    return loudness


def assign_block(rng, own, number, rows, count, top, most, skew):
    ranking = jax.random.permutation(rng, count)
    packed, ordinary = shares(count, rows * top, most, skew, True), shares(count, rows * top, most, skew, False)
    places = jnp.arange(count)

    def named(tallies, offset_by):
        used = int((tallies > 0).sum())
        fixed = max(1, used // 4)
        passed = fixed + (places - fixed + offset_by * (used - fixed)) % max(1, count - fixed)
        return jnp.zeros((count,), jnp.int32).at[ranking[jnp.where(places < fixed, places, passed)]].set(jnp.asarray(tallies, jnp.int32))

    tallies = jnp.where(number % 4 == 0, named(packed, number // 4), named(ordinary, number - number // 4 - 1))
    mixed = jax.random.permutation(jax.random.fold_in(own, 3), count)
    donor, taker = mixed[0:count // 2 * 2:2], mixed[1:count // 2 * 2:2]
    slack = jnp.minimum(tallies[donor] - 1, most - tallies[taker]) // 2
    slack = jnp.where((donor == ranking[0]) | (taker == ranking[0]) | (tallies[taker] == 0), 0, jnp.maximum(slack, 0))
    passed = jax.random.randint(jax.random.fold_in(own, 4), (count // 2,), 0, 1 << 20) % (slack + 1)
    tallies = tallies.at[donor].add(-passed).at[taker].add(passed)
    items = jnp.searchsorted(jnp.cumsum(tallies), jnp.arange(rows * top), side="right").astype(jnp.int32)
    listing = items.reshape(top, rows).T
    listing = listing[jax.random.permutation(jax.random.fold_in(own, 1), rows)]
    offset_by = jax.random.randint(jax.random.fold_in(own, 2), (rows, 1), 0, top)
    return jnp.take_along_axis(listing, (jnp.arange(top)[None, :] + offset_by) % top, axis=1)


def shares(count, total, most, skew, full):
    loads = [(1 << 20) // math.isqrt(grade ** skew) + 1 for grade in range(1, count + 1)]
    largest = most if full else min(most, max(-(-total // count), total * loads[0] // sum(loads)))
    least = 1 if total - largest >= count - 1 else 0
    holding, surplus = [largest] + [least] * (count - 1), total - largest - least * (count - 1)
    while surplus > 0:
        free = [i for i in range(1, count) if holding[i] < largest] or [i for i in range(1, count) if holding[i] < most]
        mass, left = sum([loads[i] for i in free]), surplus
        for i in free:
            more = min(most - holding[i], max(1, left * loads[i] // mass), surplus)
            holding[i] = holding[i] + more
            surplus = surplus - more
    return np.array(holding)


def normal_values(own_key, shape, scale, reach, cuts=(), kind=jnp.bfloat16):
    factor_of = block_scale(own_key, shape, cuts, -0.22, 0.18) if cuts else 1.0
    array = jax.random.normal(own_key, shape, jnp.float32) * scale * factor_of
    return jnp.minimum(jnp.maximum(array, -reach), reach).astype(kind)


def setup_inputs(seed: int = 0) -> dict:
    splits = jax.random.split(jax.random.key(seed), 11)
    train_x = normal_values(splits[0], (TRAIN, D), 1.0, 6.0, ((0, 512),))
    train_grad = normal_values(splits[1], (TRAIN, TOP, FF), 0.02, 0.119628906, ((0, 512),))
    train_routes_keys = jax.random.split(jax.random.fold_in(splits[2], 1), TRAIN // TOK_DEV)
    train_routes_turns = jax.random.permutation(jax.random.fold_in(splits[2], 3), TRAIN // TOK_DEV)
    train_routes = jax.vmap(lambda own, number: assign_block(jax.random.fold_in(splits[2], 2), own, number, TOK_DEV, EXPERTS, TOP, CAP, 2))(train_routes_keys, train_routes_turns).reshape((TRAIN, TOP))
    train_weight = jnp.clip(jnp.exp(math.log(1.0) - 2.9957323 * jax.random.uniform(splits[3], (TRAIN, TOP), jnp.float32) ** block_scale(splits[3], (TRAIN, TOP), ((0, 512),), -0.2, 0.2)), 0.05, 1.0)
    train_example = set_ends(jax.random.randint(splits[4], (TRAIN,), 0, EX_DEV), jax.random.fold_in(splits[4], 1), 0, EX_DEV - 1).astype(jnp.int32)
    probe_x = normal_values(splits[5], (PROBE, D), 1.0, 6.0, ((0, 16),))
    probe_grad = normal_values(splits[6], (PROBE, TOP, FF), 0.02, 0.119628906, ((0, 16),))
    probe_routes_keys = jax.random.split(jax.random.fold_in(splits[7], 1), PROBE // P_ROW)
    probe_routes_turns = jax.random.permutation(jax.random.fold_in(splits[7], 3), PROBE // P_ROW)
    probe_routes = jax.vmap(lambda own, number: assign_block(jax.random.fold_in(splits[7], 2), own, number, P_ROW, EXPERTS, TOP, PCAP, 2))(probe_routes_keys, probe_routes_turns).reshape((PROBE, TOP))
    probe_weight = jnp.clip(jnp.exp(math.log(1.0) - 2.9957323 * jax.random.uniform(splits[8], (PROBE, TOP), jnp.float32) ** block_scale(splits[8], (PROBE, TOP), ((0, 16),), -0.2, 0.2)), 0.05, 1.0)
    probe_example = set_ends(jax.random.randint(splits[9], (PROBE,), 0, PEX_ROW), jax.random.fold_in(splits[9], 1), 0, PEX_ROW - 1).astype(jnp.int32)
    return dict(train_x=train_x, train_grad=train_grad, train_routes=train_routes, train_weight=train_weight, train_example=train_example, probe_x=probe_x, probe_grad=probe_grad, probe_routes=probe_routes, probe_weight=probe_weight, probe_example=probe_example)


def slot_table(flat_routes, first_expert, group_size, capacity):
    route_total = flat_routes.shape[0]
    relative = flat_routes - first_expert
    member = relative[:, None] == jnp.arange(group_size, dtype=jnp.int32)[None, :]
    rank_table = jnp.cumsum(member.astype(jnp.int32), axis=0) - 1
    own_rank = jnp.sum(jnp.where(member, rank_table, 0), axis=1).astype(jnp.int32)
    inside = (relative >= 0) & (relative < group_size)
    target = jnp.where(inside, relative * capacity + own_rank, group_size * capacity).astype(jnp.int32)
    slot_index = jnp.full((group_size * capacity + 1,), -1, jnp.int32)
    slot_index = slot_index.at[target].set(jnp.arange(route_total, dtype=jnp.int32))
    return slot_index[:group_size * capacity]


def expert_tables(routes, blocks, block_rows, capacity):
    tables = lax.map(partial(slot_table, first_expert=0, group_size=EXPERTS, capacity=capacity), routes.reshape(blocks, block_rows * TOP))
    base = (jnp.arange(blocks, dtype=jnp.int32) * (block_rows * TOP))[:, None]
    tables = jnp.where(tables >= 0, tables + base, -1).astype(jnp.int32)
    return tables.reshape(blocks, EXPERTS, capacity).transpose(1, 0, 2).reshape(EXPERTS, blocks * capacity)


def reference(train_x, train_grad, train_routes, train_weight, train_example, probe_x, probe_grad, probe_routes, probe_weight, probe_example):
    devices = N_DP * N_EXPERT
    train_scaled = (train_weight[:, :, None] * train_grad.astype(jnp.float32)).astype(jnp.bfloat16).reshape(TRAIN * TOP, FF)
    probe_scaled = (probe_weight[:, :, None] * probe_grad.astype(jnp.float32)).astype(jnp.bfloat16).reshape(PROBE * TOP, FF)
    train_tables = expert_tables(train_routes, devices, TOK_DEV, CAP)
    probe_tables = expert_tables(probe_routes, N_DP, P_ROW, PCAP)
    train_owner = ((jnp.arange(TRAIN, dtype=jnp.int32) // TOK_DEV) * EX_DEV + train_example).astype(jnp.int32)
    probe_owner = ((jnp.arange(PROBE, dtype=jnp.int32) // P_ROW) * PEX_ROW + probe_example).astype(jnp.int32)

    def expert_step(running, slot_pairs):
        train_slots, probe_slots = slot_pairs
        train_valid = train_slots >= 0
        train_safe = jnp.maximum(train_slots, 0)
        probe_valid = probe_slots >= 0
        probe_safe = jnp.maximum(probe_slots, 0)
        x_rows = jnp.where(train_valid[:, None], train_x[train_safe // TOP], 0)
        g_rows = jnp.where(train_valid[:, None], train_scaled[train_safe], 0)
        y_rows = jnp.where(probe_valid[:, None], probe_x[probe_safe // TOP], 0)
        h_rows = jnp.where(probe_valid[:, None], probe_scaled[probe_safe], 0)
        feature_gram = jnp.dot(x_rows, y_rows.T, preferred_element_type=jnp.float32)
        grad_gram = jnp.dot(g_rows, h_rows.T, preferred_element_type=jnp.float32)
        pair_values = feature_gram * grad_gram
        probe_marks = ((probe_owner[probe_safe // TOP][:, None] == jnp.arange(PROBE_EX, dtype=jnp.int32)[None, :]) & probe_valid[:, None]).astype(jnp.float32)
        per_probe = jnp.dot(pair_values, probe_marks, precision=lax.Precision.HIGHEST)
        per_probe = jnp.where(train_valid[:, None], per_probe, 0.0)
        running = running + jax.ops.segment_sum(per_probe, train_owner[train_safe // TOP], TRAIN_EX)
        return running, None

    start_value = jnp.zeros((TRAIN_EX, PROBE_EX), jnp.float32)
    scores, unused = lax.scan(expert_step, start_value, (train_tables, probe_tables))
    return scores
```

```python
import jax
import jax.numpy as jnp
from jax import lax
from jax.experimental import pallas as pl
from jax.experimental.pallas import tpu as pltpu
from jax.sharding import PartitionSpec as P

MESH = pl.DeviceIdType.MESH
BF = jnp.bfloat16
F32 = jnp.float32

LANE = 128
TOK = 128
PROW = 64
TOP = 6
D = 5120
FF = 1536
NZ = 16
NR = 4
SLOTS = 8
OWN = 8
PEX_ROW = 8
EX_DEV = 4

XP = D // LANE
GP = FF // LANE
X0 = 1
G0 = X0 + XP
PANELS = G0 + GP * TOP
ALONE = 1 + 8
PART = (PANELS - ALONE) // (2 * NR)
HALF = (PART + 1) // 2


def nt(a, b):
    return lax.dot_general(a, b, (((1,), (1,)), ((), ())), preferred_element_type=F32)


def split(v):
    hi = v.astype(BF)
    return hi, (v - hi.astype(F32)).astype(BF)


def kernel(
    tx_hbm,
    tg_hbm,
    tr_ref,
    tw_ref,
    te_ref,
    px_hbm,
    pg_hbm,
    pr_ref,
    pw_ref,
    pe_ref,
    out_ref,
    slots,
    tx,
    tg,
    rawg,
    ids,
    marks,
    square,
    pmarks,
    xs,
    acc,
    rbuf,
    lsem,
    zs,
    zr,
    rs,
    rr,
    es,
    er,
):
    z = lax.axis_index("dp")
    e = lax.axis_index("expert")
    core = e % 2
    xi = (e // 2) % NR
    yi = e // (2 * NR)

    def at(dz, dx, dy):
        zz = (z + NZ + dz) % NZ
        xx = (xi + NR + dx) % NR
        yy = (yi + NR + dy) % NR
        return (zz, (yy * NR + xx) * 2 + core)

    other = (z, e + 1 - 2 * core)
    up = jnp.where(core == 0, -1, 1)
    znext = at(up, 0, 0)
    sides = ((at(0, 1, 0), at(0, -1, 0)), (at(0, 0, 1), at(0, 0, -1)))
    rank = (xi, yi)
    base = (ALONE, ALONE + NR * PART)
    own = jnp.where(core == 0, OWN, 0)
    first = jnp.where(core == 0, 0, 1)

    barrier = pltpu.get_barrier_semaphore()
    greeted = (at(1, 0, 0), at(-1, 0, 0), at(0, 1, 0), at(0, -1, 0), at(0, 0, 1), at(0, 0, -1), other)
    for who in greeted:
        pl.semaphore_signal(barrier, inc=1, device_id=who, device_id_type=MESH)

    probe_load = pltpu.make_async_copy(pg_hbm, rawg, lsem.at[0])
    probe_load.start()

    @pl.loop(0, XP)
    def _(c):
        cols = pl.ds(pl.multiple_of(c * LANE, LANE), LANE)
        pltpu.make_async_copy(px_hbm.at[:, cols], slots.at[own, X0 + c], lsem.at[1]).start()

    grad_load = pltpu.make_async_copy(tg_hbm, tg.at[0], lsem.at[2])
    grad_load.start()
    x_load = pltpu.make_async_copy(tx_hbm, tx.at[0], lsem.at[3])
    x_load.start()

    lane = lax.broadcasted_iota(jnp.int32, (1, LANE), 1)
    square[...] = jnp.zeros_like(square)
    square[0:TOP, 0:PROW] = pr_ref[...].astype(F32)
    square[TOP : TOP + 1, 0:PROW] = pe_ref[...].astype(F32)
    square[8 : 8 + TOP, 0:PROW] = pw_ref[...]
    near = square[0:8, :]
    far = pltpu.roll(near, PROW, 1)
    pmarks[...] = jnp.zeros_like(pmarks)
    for g in range(TOP // 2):
        pmarks[g : g + 1, :] = jnp.where(lane < PROW, near[2 * g : 2 * g + 1, :], far[2 * g + 1 : 2 * g + 2, :])
    owner = jnp.where(lane < PROW, near[TOP : TOP + 1, :], far[TOP : TOP + 1, :])
    pmarks[3:4, :] = owner + (z * PEX_ROW).astype(F32)
    slots[own, 0] = pmarks[...].astype(BF)

    turned = jnp.transpose(square[...])
    probe_load.wait()
    for q in range(TOP):
        scale = jnp.broadcast_to(turned[0:PROW, 8 + q : 9 + q], (PROW, LANE))
        for k in range(GP):
            block = rawg[q, :, k * LANE : (k + 1) * LANE].astype(F32)
            slots[own, G0 + k * TOP + q] = (block * scale).astype(BF)
    pltpu.make_async_copy(
        slots.at[own, pl.ds(X0, XP)], slots.at[own, pl.ds(X0, XP)], lsem.at[1]
    ).wait()

    def share(slot, axis, who, begin, count):
        return slots.at[slot, pl.ds(base[axis] + PART * who + begin, count)]

    def zcopies(src, dst):
        out = []
        for axis in range(2):
            out.append(
                pltpu.make_async_remote_copy(
                    src_ref=share(src, axis, rank[axis], 0, PART),
                    dst_ref=share(dst, axis, rank[axis], 0, PART),
                    send_sem=zs.at[dst, axis],
                    recv_sem=zr.at[dst, axis],
                    device_id=znext,
                    device_id_type=MESH,
                )
            )
        out.append(
            pltpu.make_async_remote_copy(
                src_ref=slots.at[src, pl.ds(0, ALONE)],
                dst_ref=slots.at[dst, pl.ds(0, ALONE)],
                send_sem=zs.at[dst, 2],
                recv_sem=zr.at[dst, 2],
                device_id=znext,
                device_id_type=MESH,
            )
        )
        return out

    def ring(slot, axis, kind):
        who = (rank[axis] + (0, 0, NR - 1, 1)[kind]) % NR
        begin, count = ((0, PART), (0, PART), (0, HALF), (HALF, PART - HALF))[kind]
        region = share(slot, axis, who, begin, count)
        return pltpu.make_async_remote_copy(
            src_ref=region,
            dst_ref=region,
            send_sem=rs.at[slot, axis, kind],
            recv_sem=rr.at[slot, axis, kind],
            device_id=sides[axis][kind % 2],
            device_id_type=MESH,
        )

    def landed(slot, axis, kind):
        who = (rank[axis] + (NR - 1, 1, NR - 2, 2)[kind]) % NR
        begin, count = ((0, PART), (0, PART), (0, HALF), (HALF, PART - HALF))[kind]
        region = share(slot, axis, who, begin, count)
        return pltpu.make_async_remote_copy(
            src_ref=region,
            dst_ref=region,
            send_sem=rs.at[slot, axis, kind],
            recv_sem=rr.at[slot, axis, kind],
            device_id=sides[axis][kind % 2],
            device_id_type=MESH,
        )

    pl.semaphore_wait(barrier, len(greeted))
    for copy in zcopies(own, first):
        copy.start()

    marks[0] = jnp.zeros((16, LANE), F32)
    marks[0, 0:TOP, :] = tr_ref[...].astype(F32)
    marks[0, TOP : TOP + 1, :] = te_ref[...].astype(F32)
    square[...] = jnp.zeros_like(square)
    square[0:TOP, :] = tr_ref[...].astype(F32)
    square[8 : 8 + TOP, :] = tw_ref[...]
    turned = jnp.transpose(square[...])
    for r in range(TOP):
        ids[0, r] = jnp.broadcast_to(turned[:, r : r + 1], (TOK, LANE))

    def swap(src, dst, which):
        return pltpu.make_async_remote_copy(
            src_ref=src,
            dst_ref=dst,
            send_sem=es.at[which],
            recv_sem=er.at[which],
            device_id=other,
            device_id_type=MESH,
        )

    swaps = (
        swap(marks.at[0], marks.at[1], 0),
        swap(tx.at[0], tx.at[1], 1),
        swap(tg.at[0], tg.at[1], 2),
    )
    swaps[0].start()
    x_load.wait()
    swaps[1].start()
    grad_load.wait()
    for r in range(TOP):
        scale = jnp.broadcast_to(turned[:, 8 + r : 9 + r], (TOK, LANE))

        @pl.loop(0, GP)
        def _(k):
            cols = pl.ds(pl.multiple_of(k * LANE, LANE), LANE)
            tg[0, r, :, cols] = (tg[0, r, :, cols].astype(F32) * scale).astype(BF)

    swaps[2].start()
    acc[...] = jnp.zeros_like(acc)
    swaps[0].wait_recv()
    square[0:16, :] = marks[1]
    turned = jnp.transpose(square[...])
    for r in range(TOP):
        ids[1, r] = jnp.broadcast_to(turned[:, r : r + 1], (TOK, LANE))
    swaps[1].wait_recv()
    swaps[2].wait_recv()

    def compute(slot):
        px = jnp.concatenate([slots[slot, X0 + c] for c in range(XP)], axis=1)
        px = jnp.concatenate([px, px], axis=0)
        xs[...] = nt(tx[...].reshape(2 * TOK, D), px).reshape(2, TOK, LANE)
        info = slots[slot, 0, 0:16, :].astype(F32)
        rows = lax.broadcasted_iota(jnp.int32, (LANE, LANE), 0).astype(F32)
        probe_marks = (rows == info[3:4, :]).astype(BF)

        @pl.loop(0, 2)
        def _(h):
            pg = jnp.concatenate(
                [
                    slots[slot, G0 + k * TOP : G0 + (k + 1) * TOP].reshape(TOP * PROW, LANE)
                    for k in range(GP)
                ],
                axis=1,
            )
            gram = nt(tg[h].reshape(TOP * TOK, FF), pg)
            total = jnp.zeros((TOK, LANE), F32)
            for r in range(TOP):
                who = ids[h, r]
                for g in range(TOP // 2):
                    part = gram[r * TOK : (r + 1) * TOK, g * LANE : (g + 1) * LANE]
                    total = total + jnp.where(who == info[g : g + 1, :], part, 0.0)
            hi, lo = split(total * xs[h])
            rows16 = lax.broadcasted_iota(jnp.int32, (16, TOK), 0).astype(F32)
            train_marks = (rows16 == marks[h, TOP : TOP + 1, :]).astype(BF)
            sums = jnp.dot(train_marks, hi, preferred_element_type=F32)
            sums = sums + jnp.dot(train_marks, lo, preferred_element_type=F32)
            hi, lo = split(sums)
            acc[h] += nt(hi, probe_marks) + nt(lo, probe_marks)

    def taken(j):
        return (core == 0) | (j >= 1)

    @pl.loop(0, SLOTS + 2)
    def _(j):
        @pl.when((j < SLOTS) & taken(j))
        def _():
            arrived = zcopies(j, j)
            onward = zcopies(j, jnp.minimum(j + 1, SLOTS - 1))
            for part in range(3):
                arrived[part].wait_recv()

                @pl.when(j < SLOTS - 1)
                def _():
                    onward[part].start()

                if part < 2:
                    ring(j, part, 0).start()
                    ring(j, part, 1).start()

        @pl.when((j >= 1) & (j < SLOTS + 1) & taken(j - 1))
        def _():
            slot = jnp.maximum(j - 1, 0)
            for kind in range(2):
                for axis in range(2):
                    landed(slot, axis, kind).wait_recv()
                    ring(slot, axis, kind + 2).start()

        @pl.when(j >= 2)
        def _():
            slot = jnp.maximum(j - 2, 0)

            @pl.when(taken(j - 2))
            def _():
                for kind in range(2, 4):
                    for axis in range(2):
                        landed(slot, axis, kind).wait_recv()

            compute(slot)

    last = swap(acc.at[1], rbuf, 3)
    last.start()
    last.wait_recv()
    out_ref[...] = acc[0, 0:EX_DEV, :] + rbuf[0:EX_DEV, :]

    last.wait_send()
    for copy in swaps:
        copy.wait_send()

    @pl.loop(0, SLOTS)
    def _(j):
        @pl.when(taken(j))
        def _():
            for copy in zcopies(j, j):
                copy.wait_send()
            for axis in range(2):
                for kind in range(4):
                    ring(j, axis, kind).wait_send()


def body(
    train_x,
    train_grad,
    train_routes,
    train_weight,
    train_example,
    probe_x,
    probe_grad,
    probe_routes,
    probe_weight,
    probe_example,
):
    hbm = pl.BlockSpec(memory_space=pl.ANY)
    vmem = pl.BlockSpec(memory_space=pltpu.VMEM)
    dma = pltpu.SemaphoreType.DMA
    return pl.pallas_call(
        kernel,
        out_shape=jax.ShapeDtypeStruct((EX_DEV, LANE), F32),
        in_specs=[hbm, hbm, vmem, vmem, vmem, hbm, hbm, vmem, vmem, vmem],
        out_specs=vmem,
        scratch_shapes=[
            pltpu.VMEM((SLOTS + 1, PANELS, PROW, LANE), BF),
            pltpu.VMEM((2, TOK, D), BF),
            pltpu.VMEM((2, TOP, TOK, FF), BF),
            pltpu.VMEM((TOP, PROW, FF), BF),
            pltpu.VMEM((2, TOP, TOK, LANE), F32),
            pltpu.VMEM((2, 16, LANE), F32),
            pltpu.VMEM((LANE, LANE), F32),
            pltpu.VMEM((PROW, LANE), F32),
            pltpu.VMEM((2, TOK, LANE), F32),
            pltpu.VMEM((2, 16, LANE), F32),
            pltpu.VMEM((16, LANE), F32),
            dma((4,)),
            dma((SLOTS, 3)),
            dma((SLOTS, 3)),
            dma((SLOTS, 2, 4)),
            dma((SLOTS, 2, 4)),
            dma((4,)),
            dma((4,)),
        ],
        compiler_params=pltpu.CompilerParams(
            collective_id=0, has_side_effects=True, vmem_limit_bytes=56 * 1024 * 1024
        ),
        cost_estimate=pl.CostEstimate(flops=16_000_000_000, bytes_accessed=6_000_000, transcendentals=0),
        name="ghost_scores",
    )(
        train_x,
        jnp.transpose(train_grad, (1, 0, 2)),
        train_routes.T,
        train_weight.T,
        train_example[None, :],
        probe_x,
        jnp.transpose(probe_grad, (1, 0, 2)),
        probe_routes.T,
        probe_weight.T,
        probe_example[None, :],
    )


def solution(mesh):
    in_specs = (
        P(("dp", "expert"), None),
        P(("dp", "expert"), None, None),
        P(("dp", "expert"), None),
        P(("dp", "expert"), None),
        P(("dp", "expert")),
        P("dp", None),
        P("dp", None, None),
        P("dp", None),
        P("dp", None),
        P("dp"),
    )
    out_specs = P(("dp", "expert"), None)
    return jax.shard_map(body, mesh=mesh, in_specs=in_specs, out_specs=out_specs, check_vma=False)
```

```python
import jax
import jax.numpy as jnp
from jax import lax
from jax.experimental import pallas as pl
from jax.experimental.pallas import tpu as pltpu
from jax.sharding import PartitionSpec as P

MESH = pl.DeviceIdType.MESH
BF = jnp.bfloat16
F32 = jnp.float32

LANE = 128
TOK = 128
PROW = 64
TOP = 6
D = 5120
FF = 1536
NZ = 16
NR = 4
SLOTS = 8
OWN = 8
PEX_ROW = 8
EX_DEV = 4

XP = D // LANE
GP = FF // LANE
X0 = 1
G0 = X0 + XP
PANELS = G0 + GP * TOP
ALONE = 1 + 8
PART = (PANELS - ALONE) // (2 * NR)
HALF = (PART + 1) // 2
LAG = 3


def nt(a, b):
    return lax.dot_general(a, b, (((1,), (1,)), ((), ())), preferred_element_type=F32)


def split(v):
    hi = v.astype(BF)
    return hi, (v - hi.astype(F32)).astype(BF)


def kernel(
    tx_hbm,
    tg_hbm,
    tr_ref,
    tw_ref,
    te_ref,
    px_hbm,
    pg_hbm,
    pr_ref,
    pw_ref,
    pe_ref,
    out_ref,
    slots,
    tx,
    tg,
    rawg,
    ids,
    marks,
    square,
    pmarks,
    xs,
    acc,
    rbuf,
    lsem,
    zs,
    zr,
    rs,
    rr,
    es,
    er,
):
    z = lax.axis_index("dp")
    e = lax.axis_index("expert")
    core = e % 2
    xi = (e // 2) % NR
    yi = e // (2 * NR)

    def at(dz, dx, dy):
        zz = (z + NZ + dz) % NZ
        xx = (xi + NR + dx) % NR
        yy = (yi + NR + dy) % NR
        return (zz, (yy * NR + xx) * 2 + core)

    other = (z, e + 1 - 2 * core)
    up = jnp.where(core == 0, -1, 1)
    znext = at(up, 0, 0)
    sides = ((at(0, 1, 0), at(0, -1, 0)), (at(0, 0, 1), at(0, 0, -1)))
    rank = (xi, yi)
    base = (ALONE, ALONE + NR * PART)
    own = jnp.where(core == 0, OWN, 0)
    first = jnp.where(core == 0, 0, 1)

    barrier = pltpu.get_barrier_semaphore()
    greeted = (at(1, 0, 0), at(-1, 0, 0), at(0, 1, 0), at(0, -1, 0), at(0, 0, 1), at(0, 0, -1), other)
    for who in greeted:
        pl.semaphore_signal(barrier, inc=1, device_id=who, device_id_type=MESH)

    probe_load = pltpu.make_async_copy(pg_hbm, rawg, lsem.at[0])
    probe_load.start()

    @pl.loop(0, XP)
    def _(c):
        cols = pl.ds(pl.multiple_of(c * LANE, LANE), LANE)
        pltpu.make_async_copy(px_hbm.at[:, cols], slots.at[own, X0 + c], lsem.at[1]).start()

    grad_load = pltpu.make_async_copy(tg_hbm, tg.at[0], lsem.at[2])
    grad_load.start()
    x_load = pltpu.make_async_copy(tx_hbm, tx.at[0], lsem.at[3])
    x_load.start()

    lane = lax.broadcasted_iota(jnp.int32, (1, LANE), 1)
    square[...] = jnp.zeros_like(square)
    square[0:TOP, 0:PROW] = pr_ref[...].astype(F32)
    square[TOP : TOP + 1, 0:PROW] = pe_ref[...].astype(F32)
    square[8 : 8 + TOP, 0:PROW] = pw_ref[...]
    near = square[0:8, :]
    far = pltpu.roll(near, PROW, 1)
    pmarks[...] = jnp.zeros_like(pmarks)
    for g in range(TOP // 2):
        pmarks[g : g + 1, :] = jnp.where(lane < PROW, near[2 * g : 2 * g + 1, :], far[2 * g + 1 : 2 * g + 2, :])
    owner = jnp.where(lane < PROW, near[TOP : TOP + 1, :], far[TOP : TOP + 1, :])
    pmarks[3:4, :] = owner + (z * PEX_ROW).astype(F32)
    slots[own, 0] = pmarks[...].astype(BF)

    turned = jnp.transpose(square[...])
    probe_load.wait()
    for q in range(TOP):
        scale = jnp.broadcast_to(turned[0:PROW, 8 + q : 9 + q], (PROW, LANE))
        for k in range(GP):
            block = rawg[q, :, k * LANE : (k + 1) * LANE].astype(F32)
            slots[own, G0 + k * TOP + q] = (block * scale).astype(BF)
    pltpu.make_async_copy(
        slots.at[own, pl.ds(X0, XP)], slots.at[own, pl.ds(X0, XP)], lsem.at[1]
    ).wait()

    def share(slot, axis, who, begin, count):
        return slots.at[slot, pl.ds(base[axis] + PART * who + begin, count)]

    def zcopies(src, dst):
        out = []
        for axis in range(2):
            out.append(
                pltpu.make_async_remote_copy(
                    src_ref=share(src, axis, rank[axis], 0, PART),
                    dst_ref=share(dst, axis, rank[axis], 0, PART),
                    send_sem=zs.at[dst, axis],
                    recv_sem=zr.at[dst, axis],
                    device_id=znext,
                    device_id_type=MESH,
                )
            )
        out.append(
            pltpu.make_async_remote_copy(
                src_ref=slots.at[src, pl.ds(0, ALONE)],
                dst_ref=slots.at[dst, pl.ds(0, ALONE)],
                send_sem=zs.at[dst, 2],
                recv_sem=zr.at[dst, 2],
                device_id=znext,
                device_id_type=MESH,
            )
        )
        return out

    def ring(slot, axis, kind):
        who = (rank[axis] + (0, 0, NR - 1, 1)[kind]) % NR
        begin, count = ((0, PART), (0, PART), (0, HALF), (HALF, PART - HALF))[kind]
        region = share(slot, axis, who, begin, count)
        return pltpu.make_async_remote_copy(
            src_ref=region,
            dst_ref=region,
            send_sem=rs.at[slot, axis, kind],
            recv_sem=rr.at[slot, axis, kind],
            device_id=sides[axis][kind % 2],
            device_id_type=MESH,
        )

    def landed(slot, axis, kind):
        who = (rank[axis] + (NR - 1, 1, NR - 2, 2)[kind]) % NR
        begin, count = ((0, PART), (0, PART), (0, HALF), (HALF, PART - HALF))[kind]
        region = share(slot, axis, who, begin, count)
        return pltpu.make_async_remote_copy(
            src_ref=region,
            dst_ref=region,
            send_sem=rs.at[slot, axis, kind],
            recv_sem=rr.at[slot, axis, kind],
            device_id=sides[axis][kind % 2],
            device_id_type=MESH,
        )

    pl.semaphore_wait(barrier, len(greeted))
    for copy in zcopies(own, first):
        copy.start()

    marks[0] = jnp.zeros((16, LANE), F32)
    marks[0, 0:TOP, :] = tr_ref[...].astype(F32)
    marks[0, TOP : TOP + 1, :] = te_ref[...].astype(F32)
    square[...] = jnp.zeros_like(square)
    square[0:TOP, :] = tr_ref[...].astype(F32)
    square[8 : 8 + TOP, :] = tw_ref[...]
    turned = jnp.transpose(square[...])
    for r in range(TOP):
        ids[0, r] = jnp.broadcast_to(turned[:, r : r + 1], (TOK, LANE))

    def swap(src, dst, which):
        return pltpu.make_async_remote_copy(
            src_ref=src,
            dst_ref=dst,
            send_sem=es.at[which],
            recv_sem=er.at[which],
            device_id=other,
            device_id_type=MESH,
        )

    swaps = (
        swap(marks.at[0], marks.at[1], 0),
        swap(tx.at[0], tx.at[1], 1),
        swap(tg.at[0], tg.at[1], 2),
    )
    swaps[0].start()
    x_load.wait()
    swaps[1].start()
    grad_load.wait()
    for r in range(TOP):
        scale = jnp.broadcast_to(turned[:, 8 + r : 9 + r], (TOK, LANE))

        @pl.loop(0, GP)
        def _(k):
            cols = pl.ds(pl.multiple_of(k * LANE, LANE), LANE)
            tg[0, r, :, cols] = (tg[0, r, :, cols].astype(F32) * scale).astype(BF)

    swaps[2].start()
    acc[...] = jnp.zeros_like(acc)

    def meet():
        swaps[0].wait_recv()
        square[0:16, :] = marks[1]
        turned = jnp.transpose(square[...])
        for r in range(TOP):
            ids[1, r] = jnp.broadcast_to(turned[:, r : r + 1], (TOK, LANE))
        swaps[1].wait_recv()
        swaps[2].wait_recv()

    def feature_gram(slot):
        px = jnp.concatenate([slots[slot, X0 + c] for c in range(XP)], axis=1)
        px = jnp.concatenate([px, px], axis=0)
        xs[...] = nt(tx[...].reshape(2 * TOK, D), px).reshape(2, TOK, LANE)

    def route_gram(slot, h):
        info = slots[slot, 0, 0:16, :].astype(F32)
        rows = lax.broadcasted_iota(jnp.int32, (LANE, LANE), 0).astype(F32)
        probe_marks = (rows == info[3:4, :]).astype(BF)
        pg = jnp.concatenate(
            [slots[slot, G0 + k * TOP : G0 + (k + 1) * TOP].reshape(TOP * PROW, LANE) for k in range(GP)],
            axis=1,
        )
        gram = nt(tg[h].reshape(TOP * TOK, FF), pg)
        total = jnp.zeros((TOK, LANE), F32)
        for r in range(TOP):
            who = ids[h, r]
            for g in range(TOP // 2):
                part = gram[r * TOK : (r + 1) * TOK, g * LANE : (g + 1) * LANE]
                total = total + jnp.where(who == info[g : g + 1, :], part, 0.0)
        hi, lo = split(total * xs[h])
        rows16 = lax.broadcasted_iota(jnp.int32, (16, TOK), 0).astype(F32)
        train_marks = (rows16 == marks[h, TOP : TOP + 1, :]).astype(BF)
        sums = jnp.dot(train_marks, hi, preferred_element_type=F32)
        sums = sums + jnp.dot(train_marks, lo, preferred_element_type=F32)
        hi, lo = split(sums)
        acc[h] += nt(hi, probe_marks) + nt(lo, probe_marks)

    def taken(j):
        return (core == 0) | (j >= 1)

    @pl.loop(0, SLOTS + LAG)
    def _(j):
        fresh = (j < SLOTS) & taken(j)
        ready = j >= LAG
        done = jnp.maximum(j - LAG, 0)

        def pass_on(part):
            @pl.when(fresh)
            def _():
                zcopies(j, j)[part].wait_recv()

                @pl.when(j < SLOTS - 1)
                def _():
                    zcopies(j, jnp.minimum(j + 1, SLOTS - 1))[part].start()

                if part < 2:
                    ring(j, part, 0).start()
                    ring(j, part, 1).start()

        pass_on(0)
        pl.when(ready)(lambda: feature_gram(done))
        pass_on(1)
        pl.when(ready)(lambda: route_gram(done, 0))
        pass_on(2)
        pl.when(j == LAG - 1)(meet)

        @pl.when((j >= 1) & (j < SLOTS + 1) & taken(j - 1))
        def _():
            slot = jnp.maximum(j - 1, 0)
            for kind in range(2):
                for axis in range(2):
                    landed(slot, axis, kind).wait_recv()
                    ring(slot, axis, kind + 2).start()

        pl.when(ready)(lambda: route_gram(done, 1))

        @pl.when((j >= 2) & (j < SLOTS + 2) & taken(j - 2))
        def _():
            slot = jnp.maximum(j - 2, 0)
            for kind in range(2, 4):
                for axis in range(2):
                    landed(slot, axis, kind).wait_recv()

    last = swap(acc.at[1], rbuf, 3)
    last.start()
    last.wait_recv()
    out_ref[...] = acc[0, 0:EX_DEV, :] + rbuf[0:EX_DEV, :]

    last.wait_send()
    for copy in swaps:
        copy.wait_send()

    @pl.loop(0, SLOTS)
    def _(j):
        @pl.when(taken(j))
        def _():
            for copy in zcopies(j, j):
                copy.wait_send()
            for axis in range(2):
                for kind in range(4):
                    ring(j, axis, kind).wait_send()


def body(
    train_x,
    train_grad,
    train_routes,
    train_weight,
    train_example,
    probe_x,
    probe_grad,
    probe_routes,
    probe_weight,
    probe_example,
):
    hbm = pl.BlockSpec(memory_space=pl.ANY)
    vmem = pl.BlockSpec(memory_space=pltpu.VMEM)
    dma = pltpu.SemaphoreType.DMA
    return pl.pallas_call(
        kernel,
        out_shape=jax.ShapeDtypeStruct((EX_DEV, LANE), F32),
        in_specs=[hbm, hbm, vmem, vmem, vmem, hbm, hbm, vmem, vmem, vmem],
        out_specs=vmem,
        scratch_shapes=[
            pltpu.VMEM((SLOTS + 1, PANELS, PROW, LANE), BF),
            pltpu.VMEM((2, TOK, D), BF),
            pltpu.VMEM((2, TOP, TOK, FF), BF),
            pltpu.VMEM((TOP, PROW, FF), BF),
            pltpu.VMEM((2, TOP, TOK, LANE), F32),
            pltpu.VMEM((2, 16, LANE), F32),
            pltpu.VMEM((LANE, LANE), F32),
            pltpu.VMEM((PROW, LANE), F32),
            pltpu.VMEM((2, TOK, LANE), F32),
            pltpu.VMEM((2, 16, LANE), F32),
            pltpu.VMEM((16, LANE), F32),
            dma((4,)),
            dma((SLOTS, 3)),
            dma((SLOTS, 3)),
            dma((SLOTS, 2, 4)),
            dma((SLOTS, 2, 4)),
            dma((4,)),
            dma((4,)),
        ],
        compiler_params=pltpu.CompilerParams(
            collective_id=0, has_side_effects=True, vmem_limit_bytes=56 * 1024 * 1024
        ),
        cost_estimate=pl.CostEstimate(flops=16_000_000_000, bytes_accessed=6_000_000, transcendentals=0),
        name="ghost_scores",
    )(
        train_x,
        jnp.transpose(train_grad, (1, 0, 2)),
        train_routes.T,
        train_weight.T,
        train_example[None, :],
        probe_x,
        jnp.transpose(probe_grad, (1, 0, 2)),
        probe_routes.T,
        probe_weight.T,
        probe_example[None, :],
    )


def solution(mesh):
    in_specs = (
        P(("dp", "expert"), None),
        P(("dp", "expert"), None, None),
        P(("dp", "expert"), None),
        P(("dp", "expert"), None),
        P(("dp", "expert")),
        P("dp", None),
        P("dp", None, None),
        P("dp", None),
        P("dp", None),
        P("dp"),
    )
    out_specs = P(("dp", "expert"), None)
    return jax.shard_map(body, mesh=mesh, in_specs=in_specs, out_specs=out_specs, check_vma=False)
```

```python
import jax
import jax.numpy as jnp
from jax import lax
from jax.experimental import pallas as pl
from jax.experimental.pallas import tpu as pltpu
from jax.sharding import PartitionSpec as P

MESH = pl.DeviceIdType.MESH
BF = jnp.bfloat16
F32 = jnp.float32

LANE = 128
TOK = 128
PROW = 64
TOP = 6
D = 5120
FF = 1536
NZ = 16
NR = 4
SLOTS = 8
OWN = SLOTS
PEX_ROW = 8
EX_DEV = 4

KH = FF // 2

XP = D // LANE
GP = KH // LANE
X0 = 1
G0 = X0 + XP
PANELS = G0 + GP * TOP
YPART = 11
XPART = 5
YBASE = PANELS - NR * YPART
XBASE = YBASE - NR * XPART
HALF = (YPART + 1) // 2
LAG = 3
PAIR = 6


def nt(a, b):
    return lax.dot_general(a, b, (((1,), (1,)), ((), ())), preferred_element_type=F32)


def split(v):
    hi = v.astype(BF)
    return hi, (v - hi.astype(F32)).astype(BF)


def kernel(
    tx_hbm,
    tg_hbm,
    tr_ref,
    tw_ref,
    te_ref,
    px_hbm,
    pg_hbm,
    pr_ref,
    pw_ref,
    pe_ref,
    out_ref,
    slots,
    tx,
    tg,
    away,
    rawg,
    ids,
    marks,
    square,
    pmarks,
    xs,
    near_sum,
    far_sum,
    back_sum,
    acc,
    rbuf,
    lsem,
    zs,
    zr,
    rs,
    rr,
    es,
    er,
    qs,
    qr,
):
    z = lax.axis_index("dp")
    e = lax.axis_index("expert")
    core = e % 2
    xi = (e // 2) % NR
    yi = e // (2 * NR)
    odd = xi % 2

    def at(zz, xx, yy, cc):
        return (zz, (yy * NR + xx) * 2 + cc)

    xp = xi + 1 - 2 * odd
    xn = (xi + NR - 1 + 2 * odd) % NR
    other = at(z, xi, yi, 1 - core)
    partner = at(z, xp, yi, core)
    across = at(z, xp, yi, 1 - core)
    beside = at(z, xn, yi, core)
    right = at(z, xi, (yi + 1) % NR, core)
    left = at(z, xi, (yi + NR - 1) % NR, core)
    above = at((z + 1) % NZ, xi, yi, core)
    below = at((z + NZ - 1) % NZ, xi, yi, core)
    znext = at((z + NZ - 1 + 2 * core) % NZ, xi, yi, core)
    own = jnp.where(core == 0, OWN, 0)
    first = jnp.where(core == 0, 0, 1)

    barrier = pltpu.get_barrier_semaphore()
    greeted = (other, partner, across, beside, right, left, above, below)
    for who in greeted:
        pl.semaphore_signal(barrier, inc=1, device_id=who, device_id_type=MESH)

    mine = pl.ds(pl.multiple_of(odd * KH, LANE), KH)
    theirs = pl.ds(pl.multiple_of((1 - odd) * KH, LANE), KH)
    probe_load = pltpu.make_async_copy(pg_hbm.at[:, :, mine], rawg, lsem.at[0])
    probe_load.start()

    @pl.loop(0, XP)
    def _(c):
        cols = pl.ds(pl.multiple_of(c * LANE, LANE), LANE)
        pltpu.make_async_copy(px_hbm.at[:, cols], slots.at[own, X0 + c], lsem.at[1]).start()

    away_load = pltpu.make_async_copy(tg_hbm.at[:, :, theirs], away, lsem.at[4])
    away_load.start()
    grad_load = pltpu.make_async_copy(tg_hbm.at[:, :, mine], tg.at[0], lsem.at[2])
    grad_load.start()
    x_load = pltpu.make_async_copy(tx_hbm, tx.at[0], lsem.at[3])
    x_load.start()

    lane = lax.broadcasted_iota(jnp.int32, (1, LANE), 1)
    square[...] = jnp.zeros_like(square)
    square[0:TOP, 0:PROW] = pr_ref[...].astype(F32)
    square[TOP : TOP + 1, 0:PROW] = pe_ref[...].astype(F32)
    square[8 : 8 + TOP, 0:PROW] = pw_ref[...]
    near = square[0:8, :]
    far = pltpu.roll(near, PROW, 1)
    pmarks[...] = jnp.zeros_like(pmarks)
    for g in range(TOP // 2):
        pmarks[g : g + 1, :] = jnp.where(lane < PROW, near[2 * g : 2 * g + 1, :], far[2 * g + 1 : 2 * g + 2, :])
    owner = jnp.where(lane < PROW, near[TOP : TOP + 1, :], far[TOP : TOP + 1, :])
    pmarks[3:4, :] = owner + (z * PEX_ROW).astype(F32)
    slots[own, 0] = pmarks[...].astype(BF)

    turned = jnp.transpose(square[...])
    probe_load.wait()
    for q in range(TOP):
        scale = jnp.broadcast_to(turned[0:PROW, 8 + q : 9 + q], (PROW, LANE))
        for k in range(GP):
            block = rawg[q, :, k * LANE : (k + 1) * LANE].astype(F32)
            slots[own, G0 + k * TOP + q] = (block * scale).astype(BF)
    pltpu.make_async_copy(slots.at[own, pl.ds(X0, XP)], slots.at[own, pl.ds(X0, XP)], lsem.at[1]).wait()

    def remote(src, dst, send, recv, who):
        return pltpu.make_async_remote_copy(
            src_ref=src, dst_ref=dst, send_sem=send, recv_sem=recv, device_id=who, device_id_type=MESH
        )

    def yshare(slot, who, begin, count):
        return slots.at[slot, pl.ds(YBASE + YPART * who + begin, count)]

    def xshare(slot, who):
        return slots.at[slot, pl.ds(XBASE + XPART * who, XPART)]

    def zcopy(src, dst, part):
        if part == 0:
            pick = lambda slot: yshare(slot, yi, 0, YPART)
        elif part == 1:
            pick = lambda slot: xshare(slot, xi)
        else:
            pick = lambda slot: slots.at[slot, pl.ds(0, XBASE)]
        return remote(pick(src), pick(dst), zs.at[dst, part], zr.at[dst, part], znext)

    def yring(slot, kind, landing=False):
        who = (0, 0, NR - 1, 1)[kind] + ((NR - 1, 1)[kind % 2] if landing else 0)
        begin, count = ((0, YPART), (0, YPART), (0, HALF), (HALF, YPART - HALF))[kind]
        region = yshare(slot, (yi + who) % NR, begin, count)
        return remote(region, region, rs.at[slot, 0, kind], rr.at[slot, 0, kind], (right, left)[kind % 2])

    def xring(slot, kind, landing=False):
        who = (xp, xn, (xi + 2) % NR)[kind] if landing else (xi, xi, xp)[kind]
        region = xshare(slot, who)
        return remote(region, region, rs.at[slot, 1, kind], rr.at[slot, 1, kind], (partner, beside, beside)[kind])

    pl.semaphore_wait(barrier, len(greeted))
    for part in range(3):
        zcopy(own, first, part).start()

    marks[0] = jnp.zeros((16, LANE), F32)
    marks[0, 0:TOP, :] = tr_ref[...].astype(F32)
    marks[0, TOP : TOP + 1, :] = te_ref[...].astype(F32)
    square[...] = jnp.zeros_like(square)
    square[0:TOP, :] = tr_ref[...].astype(F32)
    square[8 : 8 + TOP, :] = tw_ref[...]
    turned = jnp.transpose(square[...])

    def scale_train(ref):
        for r in range(TOP):
            scale = jnp.broadcast_to(turned[:, 8 + r : 9 + r], (TOK, LANE))

            @pl.loop(0, GP)
            def _(k):
                cols = pl.ds(pl.multiple_of(k * LANE, LANE), LANE)
                ref[r, :, cols] = (ref[r, :, cols].astype(F32) * scale).astype(BF)

    def spread(group):
        square[0:16, :] = marks[group]
        columns = jnp.transpose(square[...])
        for r in range(TOP):
            ids[group, r] = jnp.broadcast_to(columns[:, r : r + 1], (TOK, LANE))

    def swap(src, dst, which, who):
        return remote(src, dst, es.at[which], er.at[which], who)

    swaps = (
        swap(marks.at[0], marks.at[1], 0, other),
        swap(marks.at[0], marks.at[2], 1, partner),
        swap(marks.at[0], marks.at[3], 2, across),
        swap(away, tg.at[2], 3, partner),
        swap(tx.at[0], tx.at[1], 4, other),
        swap(tg.at[0], tg.at[1], 5, other),
        swap(tg.at[2], tg.at[3], 6, other),
    )
    away_load.wait()
    scale_train(away)
    swaps[3].start()
    for which in range(3):
        swaps[which].start()
    x_load.wait()
    swaps[4].start()
    grad_load.wait()
    scale_train(tg.at[0])
    swaps[5].start()
    spread(0)

    def meet_core():
        swaps[0].wait_recv()
        spread(1)
        swaps[4].wait_recv()
        swaps[5].wait_recv()

    def meet_partner():
        swaps[3].wait_recv()
        swaps[6].start()
        for group in (2, 3):
            swaps[group - 1].wait_recv()
            spread(group)

    def feature_gram(slot):
        px = jnp.concatenate([slots[slot, X0 + c] for c in range(XP)], axis=1)
        px = jnp.concatenate([px, px], axis=0)
        gram = nt(tx[...].reshape(2 * TOK, D), px)
        xs[slot] = jnp.where(lane < PROW, gram[0:TOK, :], gram[TOK : 2 * TOK, :])

    def route_gram(slot, chip):
        info = slots[slot, 0, 0:16, :].astype(F32)
        pg = jnp.concatenate(
            [slots[slot, G0 + k * TOP : G0 + (k + 1) * TOP].reshape(TOP * PROW, LANE) for k in range(GP)],
            axis=1,
        )
        gram = nt(tg[2 * chip : 2 * chip + 2].reshape(2 * TOP * TOK, KH), pg)
        sums = []
        for h in range(2):
            total = jnp.zeros((TOK, LANE), F32)
            for r in range(TOP):
                who = ids[2 * chip + h, r]
                row = (h * TOP + r) * TOK
                for g in range(TOP // 2):
                    part = gram[row : row + TOK, g * LANE : (g + 1) * LANE]
                    total = total + jnp.where(who == info[g : g + 1, :], part, 0.0)
            sums.append(total + pltpu.roll(total, PROW, 1))
        return jnp.where(lane < PROW, sums[0], sums[1])

    def give_back(slot):
        return remote(far_sum.at[slot], back_sum.at[slot], qs.at[slot], qr.at[slot], partner)

    def own_tokens(slot):
        near_sum[slot] = route_gram(slot, 0)

    def taken(j):
        return (core == 0) | (j >= 1)

    @pl.loop(0, SLOTS + LAG)
    def _(j):
        fresh = (j < SLOTS) & taken(j)
        ready = j >= LAG
        done = jnp.maximum(j - LAG, 0)

        def pass_on(part):
            @pl.when(fresh)
            def _():
                zcopy(j, j, part).wait_recv()

                @pl.when(j < SLOTS - 1)
                def _():
                    zcopy(j, jnp.minimum(j + 1, SLOTS - 1), part).start()

                if part == 0:
                    yring(j, 0).start()
                    yring(j, 1).start()
                if part == 1:
                    xring(j, 0).start()
                    xring(j, 1).start()

        pass_on(0)
        pl.when(ready)(lambda: feature_gram(done))
        pass_on(1)

        @pl.when(j >= PAIR)
        def _():
            @pl.when(j == PAIR)
            def _():
                swaps[6].wait_recv()

            late = 2 * (j - PAIR)
            begin = jnp.where(late < j - LAG, late, j - LAG)
            end = jnp.where(late < j - LAG, late + 2, j - LAG + 1)

            @pl.loop(begin, end)
            def _(slot):
                far_sum[slot] = route_gram(slot, 1).astype(BF)
                give_back(slot).start()

        pass_on(2)
        pl.when(j == LAG - 1)(meet_core)
        pl.when(j == PAIR - 1)(meet_partner)

        @pl.when((j >= 1) & (j < SLOTS + 1) & taken(j - 1))
        def _():
            slot = jnp.maximum(j - 1, 0)
            for kind in range(2):
                yring(slot, kind, True).wait_recv()
                yring(slot, kind + 2).start()
                if kind == 0:
                    xring(slot, 0, True).wait_recv()
                    xring(slot, 2).start()

        pl.when(ready)(lambda: own_tokens(done))

        @pl.when((j >= 2) & (j < SLOTS + 2) & taken(j - 2))
        def _():
            slot = jnp.maximum(j - 2, 0)
            for kind in range(2, 4):
                yring(slot, kind, True).wait_recv()
            for kind in range(1, 3):
                xring(slot, kind, True).wait_recv()

    values, owners = [], []
    rows = lax.broadcasted_iota(jnp.int32, (LANE, LANE), 0).astype(F32)
    for slot in range(SLOTS):
        give_back(slot).wait_recv()
        values.append((near_sum[slot] + back_sum[slot].astype(F32)) * xs[slot])
        owners.append((rows == slots[slot, 0, 0:16, :].astype(F32)[3:4, :]).astype(BF))
    hi, lo = split(jnp.concatenate(values, axis=1))
    owners = jnp.concatenate(owners, axis=1)
    eights = lax.broadcasted_iota(jnp.int32, (8, TOK), 0).astype(F32)
    examples = [(eights == marks[h, TOP : TOP + 1, :]).astype(F32) for h in range(2)]
    examples = jnp.concatenate(examples, axis=0).astype(BF)
    sums = jnp.dot(examples, hi, preferred_element_type=F32) + jnp.dot(examples, lo, preferred_element_type=F32)
    shape = (16, SLOTS * LANE)
    first_core = lax.broadcasted_iota(jnp.int32, shape, 0) < 8
    first_half = lax.broadcasted_iota(jnp.int32, shape, 1) % LANE < PROW
    hi, lo = split(jnp.where(first_core == first_half, sums, 0.0))
    acc[...] = nt(hi, owners) + nt(lo, owners)

    last = swap(acc.at[pl.ds(8, 8)], rbuf, 7, other)
    last.start()
    last.wait_recv()
    out_ref[...] = acc[0:EX_DEV, :] + rbuf[0:EX_DEV, :]

    last.wait_send()
    for copy in swaps:
        copy.wait_send()

    @pl.loop(0, SLOTS)
    def _(j):
        give_back(j).wait_send()

        @pl.when(taken(j))
        def _():
            for part in range(3):
                zcopy(j, j, part).wait_send()
            for kind in range(4):
                yring(j, kind).wait_send()
            for kind in range(3):
                xring(j, kind).wait_send()


def body(
    train_x,
    train_grad,
    train_routes,
    train_weight,
    train_example,
    probe_x,
    probe_grad,
    probe_routes,
    probe_weight,
    probe_example,
):
    hbm = pl.BlockSpec(memory_space=pl.ANY)
    vmem = pl.BlockSpec(memory_space=pltpu.VMEM)
    dma = pltpu.SemaphoreType.DMA
    return pl.pallas_call(
        kernel,
        out_shape=jax.ShapeDtypeStruct((EX_DEV, LANE), F32),
        in_specs=[hbm, hbm, vmem, vmem, vmem, hbm, hbm, vmem, vmem, vmem],
        out_specs=vmem,
        scratch_shapes=[
            pltpu.VMEM((SLOTS + 1, PANELS, PROW, LANE), BF),
            pltpu.VMEM((2, TOK, D), BF),
            pltpu.VMEM((4, TOP, TOK, KH), BF),
            pltpu.VMEM((TOP, TOK, KH), BF),
            pltpu.VMEM((TOP, PROW, KH), BF),
            pltpu.VMEM((4, TOP, TOK, LANE), F32),
            pltpu.VMEM((4, 16, LANE), F32),
            pltpu.VMEM((LANE, LANE), F32),
            pltpu.VMEM((PROW, LANE), F32),
            pltpu.VMEM((SLOTS, TOK, LANE), F32),
            pltpu.VMEM((SLOTS, TOK, LANE), F32),
            pltpu.VMEM((SLOTS, TOK, LANE), BF),
            pltpu.VMEM((SLOTS, TOK, LANE), BF),
            pltpu.VMEM((16, LANE), F32),
            pltpu.VMEM((8, LANE), F32),
            dma((5,)),
            dma((SLOTS, 3)),
            dma((SLOTS, 3)),
            dma((SLOTS, 2, 4)),
            dma((SLOTS, 2, 4)),
            dma((8,)),
            dma((8,)),
            dma((SLOTS,)),
            dma((SLOTS,)),
        ],
        compiler_params=pltpu.CompilerParams(
            collective_id=0, has_side_effects=True, vmem_limit_bytes=56 * 1024 * 1024
        ),
        cost_estimate=pl.CostEstimate(flops=16_000_000_000, bytes_accessed=6_000_000, transcendentals=0),
        name="ghost_scores",
    )(
        train_x,
        jnp.transpose(train_grad, (1, 0, 2)),
        train_routes.T,
        train_weight.T,
        train_example[None, :],
        probe_x,
        jnp.transpose(probe_grad, (1, 0, 2)),
        probe_routes.T,
        probe_weight.T,
        probe_example[None, :],
    )


def solution(mesh):
    in_specs = (
        P(("dp", "expert"), None),
        P(("dp", "expert"), None, None),
        P(("dp", "expert"), None),
        P(("dp", "expert"), None),
        P(("dp", "expert")),
        P("dp", None),
        P("dp", None, None),
        P("dp", None),
        P("dp", None),
        P("dp"),
    )
    out_specs = P(("dp", "expert"), None)
    return jax.shard_map(body, mesh=mesh, in_specs=in_specs, out_specs=out_specs, check_vma=False)
```

```python
import jax
import jax.numpy as jnp
from jax import lax
from jax.experimental import pallas as pl
from jax.experimental.pallas import tpu as pltpu
from jax.sharding import PartitionSpec as P

MESH = pl.DeviceIdType.MESH
BF = jnp.bfloat16
F32 = jnp.float32

LANE = 128
TOK = 128
PROW = 64
TOP = 6
D = 5120
FF = 1536
NZ = 16
NR = 4
SLOTS = 8
OWN = 8
PEX_ROW = 8
EX_DEV = 4

XP = D // LANE
GP = FF // LANE
X0 = 1
G0 = X0 + XP
PANELS = G0 + GP * TOP
ALONE = 1 + 8
PART = (PANELS - ALONE) // (2 * NR)
HALF = (PART + 1) // 2
LAG = 4


def nt(a, b):
    return lax.dot_general(a, b, (((1,), (1,)), ((), ())), preferred_element_type=F32)


def split(v):
    hi = v.astype(BF)
    return hi, (v - hi.astype(F32)).astype(BF)


def kernel(
    tx_hbm,
    tg_hbm,
    tr_ref,
    tw_ref,
    te_ref,
    px_hbm,
    pg_hbm,
    pr_ref,
    pw_ref,
    pe_ref,
    out_ref,
    slots,
    tx,
    tg,
    rawg,
    ids,
    marks,
    square,
    pmarks,
    xs,
    acc,
    rbuf,
    lsem,
    zs,
    zr,
    rs,
    rr,
    es,
    er,
):
    z = lax.axis_index("dp")
    e = lax.axis_index("expert")
    core = e % 2
    xi = (e // 2) % NR
    yi = e // (2 * NR)

    def at(dz, dx, dy):
        zz = (z + NZ + dz) % NZ
        xx = (xi + NR + dx) % NR
        yy = (yi + NR + dy) % NR
        return (zz, (yy * NR + xx) * 2 + core)

    other = (z, e + 1 - 2 * core)
    up = jnp.where(core == 0, -1, 1)
    znext = at(up, 0, 0)
    sides = ((at(0, 1, 0), at(0, -1, 0)), (at(0, 0, 1), at(0, 0, -1)))
    rank = (xi, yi)
    base = (ALONE, ALONE + NR * PART)
    own = jnp.where(core == 0, OWN, 0)
    first = jnp.where(core == 0, 0, 1)

    barrier = pltpu.get_barrier_semaphore()
    greeted = (at(1, 0, 0), at(-1, 0, 0), at(0, 1, 0), at(0, -1, 0), at(0, 0, 1), at(0, 0, -1), other)
    for who in greeted:
        pl.semaphore_signal(barrier, inc=1, device_id=who, device_id_type=MESH)

    probe_load = pltpu.make_async_copy(pg_hbm, rawg, lsem.at[0])
    probe_load.start()

    @pl.loop(0, XP)
    def _(c):
        cols = pl.ds(pl.multiple_of(c * LANE, LANE), LANE)
        pltpu.make_async_copy(px_hbm.at[:, cols], slots.at[own, X0 + c], lsem.at[1]).start()

    grad_load = pltpu.make_async_copy(tg_hbm, tg.at[0], lsem.at[2])
    grad_load.start()
    x_load = pltpu.make_async_copy(tx_hbm, tx.at[0], lsem.at[3])
    x_load.start()

    lane = lax.broadcasted_iota(jnp.int32, (1, LANE), 1)
    square[...] = jnp.zeros_like(square)
    square[0:TOP, 0:PROW] = pr_ref[...].astype(F32)
    square[TOP : TOP + 1, 0:PROW] = pe_ref[...].astype(F32)
    square[8 : 8 + TOP, 0:PROW] = pw_ref[...]
    near = square[0:8, :]
    both = near + pltpu.roll(near, PROW, 1)
    pmarks[...] = jnp.zeros_like(pmarks)
    pmarks[0:TOP, :] = both[0:TOP, :]
    pmarks[TOP : TOP + 1, :] = both[TOP : TOP + 1, :] + (z * PEX_ROW).astype(F32)
    slots[own, 0] = pmarks[...].astype(BF)

    turned = jnp.transpose(square[...])
    probe_load.wait()
    for q in range(TOP):
        scale = jnp.broadcast_to(turned[0:PROW, 8 + q : 9 + q], (PROW, LANE))
        for k in range(GP):
            block = rawg[q, :, k * LANE : (k + 1) * LANE].astype(F32)
            slots[own, G0 + k * TOP + q] = (block * scale).astype(BF)
    pltpu.make_async_copy(
        slots.at[own, pl.ds(X0, XP)], slots.at[own, pl.ds(X0, XP)], lsem.at[1]
    ).wait()

    def share(slot, axis, who, begin, count):
        return slots.at[slot, pl.ds(base[axis] + PART * who + begin, count)]

    def zcopies(src, dst):
        out = []
        for axis in range(2):
            out.append(
                pltpu.make_async_remote_copy(
                    src_ref=share(src, axis, rank[axis], 0, PART),
                    dst_ref=share(dst, axis, rank[axis], 0, PART),
                    send_sem=zs.at[dst, axis],
                    recv_sem=zr.at[dst, axis],
                    device_id=znext,
                    device_id_type=MESH,
                )
            )
        out.append(
            pltpu.make_async_remote_copy(
                src_ref=slots.at[src, pl.ds(0, ALONE)],
                dst_ref=slots.at[dst, pl.ds(0, ALONE)],
                send_sem=zs.at[dst, 2],
                recv_sem=zr.at[dst, 2],
                device_id=znext,
                device_id_type=MESH,
            )
        )
        return out

    def ring(slot, axis, kind):
        who = (rank[axis] + (0, 0, NR - 1, 1)[kind]) % NR
        begin, count = ((0, PART), (0, PART), (0, HALF), (HALF, PART - HALF))[kind]
        region = share(slot, axis, who, begin, count)
        return pltpu.make_async_remote_copy(
            src_ref=region,
            dst_ref=region,
            send_sem=rs.at[slot, axis, kind],
            recv_sem=rr.at[slot, axis, kind],
            device_id=sides[axis][kind % 2],
            device_id_type=MESH,
        )

    def landed(slot, axis, kind):
        who = (rank[axis] + (NR - 1, 1, NR - 2, 2)[kind]) % NR
        begin, count = ((0, PART), (0, PART), (0, HALF), (HALF, PART - HALF))[kind]
        region = share(slot, axis, who, begin, count)
        return pltpu.make_async_remote_copy(
            src_ref=region,
            dst_ref=region,
            send_sem=rs.at[slot, axis, kind],
            recv_sem=rr.at[slot, axis, kind],
            device_id=sides[axis][kind % 2],
            device_id_type=MESH,
        )

    pl.semaphore_wait(barrier, len(greeted))
    for copy in zcopies(own, first):
        copy.start()

    marks[0] = jnp.zeros((16, LANE), F32)
    marks[0, 0:TOP, :] = tr_ref[...].astype(F32)
    marks[0, TOP : TOP + 1, :] = te_ref[...].astype(F32)
    square[...] = jnp.zeros_like(square)
    square[0:TOP, :] = tr_ref[...].astype(F32)
    square[8 : 8 + TOP, :] = tw_ref[...]
    turned = jnp.transpose(square[...])
    for r in range(TOP):
        ids[0, r] = jnp.broadcast_to(turned[:, r : r + 1], (TOK, LANE))

    def swap(src, dst, which):
        return pltpu.make_async_remote_copy(
            src_ref=src,
            dst_ref=dst,
            send_sem=es.at[which],
            recv_sem=er.at[which],
            device_id=other,
            device_id_type=MESH,
        )

    swaps = (
        swap(marks.at[0], marks.at[1], 0),
        swap(tx.at[0], tx.at[1], 1),
        swap(tg.at[0], tg.at[1], 2),
    )
    swaps[0].start()
    x_load.wait()
    swaps[1].start()
    grad_load.wait()
    for r in range(TOP):
        scale = jnp.broadcast_to(turned[:, 8 + r : 9 + r], (TOK, LANE))

        @pl.loop(0, GP)
        def _(k):
            cols = pl.ds(pl.multiple_of(k * LANE, LANE), LANE)
            tg[0, r, :, cols] = (tg[0, r, :, cols].astype(F32) * scale).astype(BF)

    swaps[2].start()
    acc[...] = jnp.zeros_like(acc)

    def meet():
        swaps[0].wait_recv()
        square[0:16, :] = marks[1]
        turned = jnp.transpose(square[...])
        for r in range(TOP):
            ids[1, r] = jnp.broadcast_to(turned[:, r : r + 1], (TOK, LANE))
        swaps[1].wait_recv()
        swaps[2].wait_recv()

    def feature_gram(pair):
        px = jnp.concatenate(
            [jnp.concatenate([slots[2 * pair + i, X0 + c] for c in range(XP)], axis=1) for i in range(2)], axis=0
        )
        xs[...] = nt(tx[...].reshape(2 * TOK, D), px).reshape(2, TOK, LANE)

    def route_gram(pair, h):
        info = [slots[2 * pair + i, 0, 0:16, :].astype(F32) for i in range(2)]
        info = jnp.where(lane < PROW, info[0], info[1])
        rows = lax.broadcasted_iota(jnp.int32, (LANE, LANE), 0).astype(F32)
        probe_marks = (rows == info[TOP : TOP + 1, :]).astype(BF)
        pg = jnp.concatenate(
            [
                jnp.concatenate(
                    [slots[2 * pair + i, G0 + k * TOP + q] for q in range(TOP) for i in range(2)], axis=0
                )
                for k in range(GP)
            ],
            axis=1,
        )
        gram = nt(tg[h].reshape(TOP * TOK, FF), pg)
        total = jnp.zeros((TOK, LANE), F32)
        for r in range(TOP):
            who = ids[h, r]
            for q in range(TOP):
                part = gram[r * TOK : (r + 1) * TOK, q * LANE : (q + 1) * LANE]
                total = total + jnp.where(who == info[q : q + 1, :], part, 0.0)
        hi, lo = split(total * xs[h])
        rows16 = lax.broadcasted_iota(jnp.int32, (16, TOK), 0).astype(F32)
        train_marks = (rows16 == marks[h, TOP : TOP + 1, :]).astype(BF)
        sums = jnp.dot(train_marks, hi, preferred_element_type=F32)
        sums = sums + jnp.dot(train_marks, lo, preferred_element_type=F32)
        hi, lo = split(sums)
        acc[h] += nt(hi, probe_marks) + nt(lo, probe_marks)

    def taken(j):
        return (core == 0) | (j >= 1)

    @pl.loop(0, SLOTS + LAG)
    def _(j):
        fresh = (j < SLOTS) & taken(j)
        ready = j >= LAG
        since = jnp.maximum(j - LAG, 0)
        pair, half = since // 2, since % 2

        def pass_on(part):
            @pl.when(fresh)
            def _():
                zcopies(j, j)[part].wait_recv()

                @pl.when(j < SLOTS - 1)
                def _():
                    zcopies(j, jnp.minimum(j + 1, SLOTS - 1))[part].start()

                if part < 2:
                    ring(j, part, 0).start()
                    ring(j, part, 1).start()

        pass_on(0)
        pl.when(ready & (half == 0))(lambda: feature_gram(pair))
        pass_on(1)
        pl.when(ready)(lambda: route_gram(pair, half))
        pass_on(2)
        pl.when(j == LAG - 1)(meet)

        @pl.when((j >= 1) & (j < SLOTS + 1) & taken(j - 1))
        def _():
            slot = jnp.maximum(j - 1, 0)
            for kind in range(2):
                for axis in range(2):
                    landed(slot, axis, kind).wait_recv()
                    ring(slot, axis, kind + 2).start()

        @pl.when((j >= 2) & (j < SLOTS + 2) & taken(j - 2))
        def _():
            slot = jnp.maximum(j - 2, 0)
            for kind in range(2, 4):
                for axis in range(2):
                    landed(slot, axis, kind).wait_recv()

    last = swap(acc.at[1], rbuf, 3)
    last.start()
    last.wait_recv()
    out_ref[...] = acc[0, 0:EX_DEV, :] + rbuf[0:EX_DEV, :]

    last.wait_send()
    for copy in swaps:
        copy.wait_send()

    @pl.loop(0, SLOTS)
    def _(j):
        @pl.when(taken(j))
        def _():
            for copy in zcopies(j, j):
                copy.wait_send()
            for axis in range(2):
                for kind in range(4):
                    ring(j, axis, kind).wait_send()


def body(
    train_x,
    train_grad,
    train_routes,
    train_weight,
    train_example,
    probe_x,
    probe_grad,
    probe_routes,
    probe_weight,
    probe_example,
):
    hbm = pl.BlockSpec(memory_space=pl.ANY)
    vmem = pl.BlockSpec(memory_space=pltpu.VMEM)
    dma = pltpu.SemaphoreType.DMA
    return pl.pallas_call(
        kernel,
        out_shape=jax.ShapeDtypeStruct((EX_DEV, LANE), F32),
        in_specs=[hbm, hbm, vmem, vmem, vmem, hbm, hbm, vmem, vmem, vmem],
        out_specs=vmem,
        scratch_shapes=[
            pltpu.VMEM((SLOTS + 1, PANELS, PROW, LANE), BF),
            pltpu.VMEM((2, TOK, D), BF),
            pltpu.VMEM((2, TOP, TOK, FF), BF),
            pltpu.VMEM((TOP, PROW, FF), BF),
            pltpu.VMEM((2, TOP, TOK, LANE), F32),
            pltpu.VMEM((2, 16, LANE), F32),
            pltpu.VMEM((LANE, LANE), F32),
            pltpu.VMEM((PROW, LANE), F32),
            pltpu.VMEM((2, TOK, LANE), F32),
            pltpu.VMEM((2, 16, LANE), F32),
            pltpu.VMEM((16, LANE), F32),
            dma((4,)),
            dma((SLOTS, 3)),
            dma((SLOTS, 3)),
            dma((SLOTS, 2, 4)),
            dma((SLOTS, 2, 4)),
            dma((4,)),
            dma((4,)),
        ],
        compiler_params=pltpu.CompilerParams(
            collective_id=0, has_side_effects=True, vmem_limit_bytes=56 * 1024 * 1024
        ),
        cost_estimate=pl.CostEstimate(flops=16_000_000_000, bytes_accessed=6_000_000, transcendentals=0),
        name="ghost_scores",
    )(
        train_x,
        jnp.transpose(train_grad, (1, 0, 2)),
        train_routes.T,
        train_weight.T,
        train_example[None, :],
        probe_x,
        jnp.transpose(probe_grad, (1, 0, 2)),
        probe_routes.T,
        probe_weight.T,
        probe_example[None, :],
    )


def solution(mesh):
    in_specs = (
        P(("dp", "expert"), None),
        P(("dp", "expert"), None, None),
        P(("dp", "expert"), None),
        P(("dp", "expert"), None),
        P(("dp", "expert")),
        P("dp", None),
        P("dp", None, None),
        P("dp", None),
        P("dp", None),
        P("dp"),
    )
    out_specs = P(("dp", "expert"), None)
    return jax.shard_map(body, mesh=mesh, in_specs=in_specs, out_specs=out_specs, check_vma=False)
```

```python
import jax
import jax.numpy as jnp
from jax import lax
from jax.experimental import pallas as pl
from jax.experimental.pallas import tpu as pltpu
from jax.sharding import PartitionSpec as P

MESH = pl.DeviceIdType.MESH
BF = jnp.bfloat16
F32 = jnp.float32

LANE = 128
TOK = 128
PROW = 64
TOP = 6
D = 5120
FF = 1536
NZ = 16
NR = 4
SLOTS = 8
OWN = SLOTS
PEX_ROW = 8
EX_DEV = 4

KQ = FF // 4
KH = FF // 2

XP = D // LANE
GP = KH // LANE
X0 = 1
G0 = X0 + XP
PANELS = G0 + GP * TOP
PARTS = (10, 6)
BASES = (PANELS - NR * PARTS[0], PANELS - NR * sum(PARTS))
PAIRS = SLOTS // 2
LAG = 4


def nt(a, b):
    return lax.dot_general(a, b, (((1,), (1,)), ((), ())), preferred_element_type=F32)


def split(v):
    hi = v.astype(BF)
    return hi, (v - hi.astype(F32)).astype(BF)


def kernel(
    tx_hbm,
    tg_hbm,
    tr_ref,
    tw_ref,
    te_ref,
    px_hbm,
    pg_hbm,
    pr_ref,
    pw_ref,
    pe_ref,
    out_ref,
    slots,
    tx,
    tg,
    tgx,
    away,
    rawg,
    ids,
    marks,
    square,
    pmarks,
    xs,
    near_sum,
    far_sum,
    back_sum,
    acc,
    rbuf,
    lsem,
    zs,
    zr,
    rs,
    rr,
    es,
    er,
    qs,
    qr,
):
    z = lax.axis_index("dp")
    e = lax.axis_index("expert")
    core = e % 2
    xi = (e // 2) % NR
    yi = e // (2 * NR)
    odd = xi % 2

    def at(zz, xx, yy, cc):
        return (zz, (yy * NR + xx) * 2 + cc)

    xr, xl = (xi + 1) % NR, (xi + NR - 1) % NR
    xp, xn = xi + 1 - 2 * odd, (xi + NR - 1 + 2 * odd) % NR
    yr, yl = (yi + 1) % NR, (yi + NR - 1) % NR
    other = at(z, xi, yi, 1 - core)
    mates = (at(z, xp, yi, core), at(z, xn, yi, core))
    across = (at(z, xp, yi, 1 - core), at(z, xn, yi, 1 - core))
    sides = ((at(z, xi, yr, core), at(z, xi, yl, core)), (at(z, xr, yi, core), at(z, xl, yi, core)))
    ranks = (yi, xi)
    above = at((z + 1) % NZ, xi, yi, core)
    below = at((z + NZ - 1) % NZ, xi, yi, core)
    znext = at((z + NZ - 1 + 2 * core) % NZ, xi, yi, core)
    own = jnp.where(core == 0, OWN, 0)
    first = jnp.where(core == 0, 0, 1)

    barrier = pltpu.get_barrier_semaphore()
    greeted = (other, *mates, *across, *sides[0], above, below)
    for who in greeted:
        pl.semaphore_signal(barrier, inc=1, device_id=who, device_id_type=MESH)

    def quarter(i):
        return pl.ds(pl.multiple_of(i * KQ, LANE), KQ)

    mine = (quarter(odd), quarter(3 - odd))
    theirs = (quarter(1 - odd), quarter(2 + odd))
    parts = (pl.ds(0, KQ), pl.ds(KQ, KQ))
    probe_load = [
        pltpu.make_async_copy(pg_hbm.at[:, :, mine[i]], rawg.at[:, :, parts[i]], lsem.at[i]) for i in range(2)
    ]
    for copy in probe_load:
        copy.start()

    @pl.loop(0, XP)
    def _(c):
        cols = pl.ds(pl.multiple_of(c * LANE, LANE), LANE)
        pltpu.make_async_copy(px_hbm.at[:, cols], slots.at[own, X0 + c], lsem.at[2]).start()

    away_load = [pltpu.make_async_copy(tg_hbm.at[:, :, theirs[i]], away.at[i], lsem.at[3 + i]) for i in range(2)]
    grad_load = [
        pltpu.make_async_copy(tg_hbm.at[:, :, mine[i]], tg.at[0, :, :, parts[i]], lsem.at[5 + i]) for i in range(2)
    ]
    for copy in away_load + grad_load:
        copy.start()
    x_load = pltpu.make_async_copy(tx_hbm, tx.at[0], lsem.at[7])
    x_load.start()

    lane = lax.broadcasted_iota(jnp.int32, (1, LANE), 1)
    square[...] = jnp.zeros_like(square)
    square[0:TOP, 0:PROW] = pr_ref[...].astype(F32)
    square[TOP : TOP + 1, 0:PROW] = pe_ref[...].astype(F32)
    square[8 : 8 + TOP, 0:PROW] = pw_ref[...]
    near = square[0:8, :]
    both = near + pltpu.roll(near, PROW, 1)
    pmarks[...] = jnp.zeros_like(pmarks)
    pmarks[0:TOP, :] = both[0:TOP, :]
    pmarks[TOP : TOP + 1, :] = both[TOP : TOP + 1, :] + (z * PEX_ROW).astype(F32)
    slots[own, 0] = pmarks[...].astype(BF)

    turned = jnp.transpose(square[...])
    for copy in probe_load:
        copy.wait()
    for q in range(TOP):
        scale = jnp.broadcast_to(turned[0:PROW, 8 + q : 9 + q], (PROW, LANE))
        for k in range(GP):
            block = rawg[q, :, k * LANE : (k + 1) * LANE].astype(F32)
            slots[own, G0 + k * TOP + q] = (block * scale).astype(BF)
    pltpu.make_async_copy(slots.at[own, pl.ds(X0, XP)], slots.at[own, pl.ds(X0, XP)], lsem.at[2]).wait()

    def remote(src, dst, send, recv, who):
        return pltpu.make_async_remote_copy(
            src_ref=src, dst_ref=dst, send_sem=send, recv_sem=recv, device_id=who, device_id_type=MESH
        )

    def share(slot, axis, who, begin, count):
        return slots.at[slot, pl.ds(BASES[axis] + PARTS[axis] * who + begin, count)]

    def zcopy(src, dst, part):
        if part < 2:
            pick = lambda slot: share(slot, part, ranks[part], 0, PARTS[part])
        else:
            pick = lambda slot: slots.at[slot, pl.ds(0, BASES[1])]
        return remote(pick(src), pick(dst), zs.at[dst, part], zr.at[dst, part], znext)

    def ring(slot, axis, kind, landing=False):
        size = PARTS[axis]
        who = (0, 0, NR - 1, 1)[kind] + ((NR - 1, 1)[kind % 2] if landing else 0)
        begin, count = ((0, size), (0, size), (0, size // 2), (size // 2, size - size // 2))[kind]
        region = share(slot, axis, (ranks[axis] + who) % NR, begin, count)
        return remote(region, region, rs.at[slot, axis, kind], rr.at[slot, axis, kind], sides[axis][kind % 2])

    pl.semaphore_wait(barrier, len(greeted))
    for part in range(3):
        zcopy(own, first, part).start()

    marks[0] = jnp.zeros((16, LANE), F32)
    marks[0, 0:TOP, :] = tr_ref[...].astype(F32)
    marks[0, TOP : TOP + 1, :] = te_ref[...].astype(F32)
    square[...] = jnp.zeros_like(square)
    square[0:TOP, :] = tr_ref[...].astype(F32)
    square[8 : 8 + TOP, :] = tw_ref[...]
    turned = jnp.transpose(square[...])

    def scale_train(ref, panels):
        for r in range(TOP):
            scale = jnp.broadcast_to(turned[:, 8 + r : 9 + r], (TOK, LANE))

            @pl.loop(0, panels)
            def _(k):
                cols = pl.ds(pl.multiple_of(k * LANE, LANE), LANE)
                ref[r, :, cols] = (ref[r, :, cols].astype(F32) * scale).astype(BF)

    def spread(group):
        square[0:16, :] = marks[group]
        columns = jnp.transpose(square[...])
        for r in range(TOP):
            ids[group, r] = jnp.broadcast_to(columns[:, r : r + 1], (TOK, LANE))

    def swap(src, dst, which, who):
        return remote(src, dst, es.at[which], er.at[which], who)

    swaps = (
        swap(marks.at[0], marks.at[1], 0, other),
        swap(marks.at[0], marks.at[2], 1, mates[0]),
        swap(marks.at[0], marks.at[3], 2, across[0]),
        swap(marks.at[0], marks.at[4], 3, mates[1]),
        swap(marks.at[0], marks.at[5], 4, across[1]),
        swap(away.at[0], tgx.at[0], 5, mates[0]),
        swap(away.at[1], tgx.at[2], 6, mates[1]),
        swap(tx.at[0], tx.at[1], 7, other),
        swap(tg.at[0], tg.at[1], 8, other),
        swap(tgx.at[0], tgx.at[1], 9, other),
        swap(tgx.at[2], tgx.at[3], 10, other),
    )
    for i in range(2):
        away_load[i].wait()
        scale_train(away.at[i], KQ // LANE)
        swaps[5 + i].start()
    for which in range(5):
        swaps[which].start()
    x_load.wait()
    swaps[7].start()
    for copy in grad_load:
        copy.wait()
    scale_train(tg.at[0], GP)
    swaps[8].start()
    spread(0)

    def meet_core():
        swaps[0].wait_recv()
        spread(1)
        swaps[7].wait_recv()
        swaps[8].wait_recv()

    def meet_mates():
        for i in range(2):
            swaps[5 + i].wait_recv()
            swaps[9 + i].start()
        for group in range(2, 6):
            swaps[group - 1].wait_recv()
            spread(group)

    def feature_gram(pair):
        px = jnp.concatenate(
            [jnp.concatenate([slots[2 * pair + i, X0 + c] for c in range(XP)], axis=1) for i in range(2)], axis=0
        )
        xs[pair] = nt(tx[...].reshape(2 * TOK, D), px).reshape(2, TOK, LANE)

    def route_gram(pair, lhs, group, panels):
        info = [slots[2 * pair + i, 0, 0:16, :].astype(F32) for i in range(2)]
        info = jnp.where(lane < PROW, info[0], info[1])
        pg = jnp.concatenate(
            [
                jnp.concatenate(
                    [slots[2 * pair + i, G0 + k * TOP + q] for q in range(TOP) for i in range(2)], axis=0
                )
                for k in panels
            ],
            axis=1,
        )
        gram = nt(lhs.reshape(TOP * TOK, len(panels) * LANE), pg)
        total = jnp.zeros((TOK, LANE), F32)
        for r in range(TOP):
            who = ids[group, r]
            for q in range(TOP):
                part = gram[r * TOK : (r + 1) * TOK, q * LANE : (q + 1) * LANE]
                total = total + jnp.where(who == info[q : q + 1, :], part, 0.0)
        return total

    def give_back(pair, i):
        return remote(far_sum.at[pair, i], back_sum.at[pair, i], qs.at[pair, i], qr.at[pair, i], mates[i])

    def own_tokens(pair):
        for h in range(2):
            near_sum[pair, h] = route_gram(pair, tg[h], h, range(GP))

    def mate_tokens(pair, i):
        for h in range(2):
            panels = range(i * GP // 2, (i + 1) * GP // 2)
            far_sum[pair, i, h] = route_gram(pair, tgx[2 * i + h], 2 + 2 * i + h, panels).astype(BF)
        give_back(pair, i).start()

    def taken(j):
        return (core == 0) | (j >= 1)

    @pl.loop(0, SLOTS + LAG)
    def _(j):
        fresh = (j < SLOTS) & taken(j)
        ready = j >= LAG
        since = jnp.maximum(j - LAG, 0)
        pair = since // 2
        at_home = (since % 2 == 0) != (pair == PAIRS - 1)

        def pass_on(part):
            @pl.when(fresh)
            def _():
                zcopy(j, j, part).wait_recv()

                @pl.when(j < SLOTS - 1)
                def _():
                    zcopy(j, jnp.minimum(j + 1, SLOTS - 1), part).start()

                if part < 2:
                    ring(j, part, 0).start()
                    ring(j, part, 1).start()

        pass_on(0)

        @pl.when(j == LAG + 1)
        def _():
            swaps[9].wait_recv()
            swaps[10].wait_recv()

        pl.when(ready & at_home)(lambda: feature_gram(pair))
        pl.when(ready & ~at_home)(lambda: mate_tokens(pair, 0))
        pass_on(1)
        pl.when(ready & at_home)(lambda: own_tokens(pair))
        pl.when(ready & ~at_home)(lambda: mate_tokens(pair, 1))
        pass_on(2)
        pl.when(j == LAG - 1)(meet_core)

        @pl.when((j >= 1) & (j < SLOTS + 1) & taken(j - 1))
        def _():
            slot = jnp.maximum(j - 1, 0)
            for kind in range(2):
                for axis in range(2):
                    ring(slot, axis, kind, True).wait_recv()
                    ring(slot, axis, kind + 2).start()

        pl.when(j == LAG)(meet_mates)

        @pl.when((j >= 2) & (j < SLOTS + 2) & taken(j - 2))
        def _():
            slot = jnp.maximum(j - 2, 0)
            for kind in range(2, 4):
                for axis in range(2):
                    ring(slot, axis, kind, True).wait_recv()

    rows = lax.broadcasted_iota(jnp.int32, (LANE, LANE), 0).astype(F32)
    rows16 = lax.broadcasted_iota(jnp.int32, (16, TOK), 0).astype(F32)
    owners, values = [], ([], [])
    for pair in range(PAIRS):
        info = [slots[2 * pair + i, 0, 0:16, :].astype(F32) for i in range(2)]
        info = jnp.where(lane < PROW, info[0], info[1])
        owners.append((rows == info[TOP : TOP + 1, :]).astype(BF))
        for i in range(2):
            give_back(pair, i).wait_recv()
        for h in range(2):
            back = back_sum[pair, 0, h].astype(F32) + back_sum[pair, 1, h].astype(F32)
            values[h].append((near_sum[pair, h] + back) * xs[pair, h])
    owners = jnp.concatenate(owners, axis=1)
    sums = []
    for h in range(2):
        hi, lo = split(jnp.concatenate(values[h], axis=1))
        examples = (rows16 == marks[h, TOP : TOP + 1, :]).astype(BF)
        part = jnp.dot(examples, hi, preferred_element_type=F32) + jnp.dot(examples, lo, preferred_element_type=F32)
        sums.append(part[0:8, :])
    hi, lo = split(jnp.concatenate(sums, axis=0))
    acc[...] = nt(hi, owners) + nt(lo, owners)

    last = swap(acc.at[pl.ds(8, 8)], rbuf, 11, other)
    last.start()
    last.wait_recv()
    out_ref[...] = acc[0:EX_DEV, :] + rbuf[0:EX_DEV, :]

    last.wait_send()
    for copy in swaps:
        copy.wait_send()

    @pl.loop(0, PAIRS)
    def _(pair):
        for i in range(2):
            give_back(pair, i).wait_send()

    @pl.loop(0, SLOTS)
    def _(j):
        @pl.when(taken(j))
        def _():
            for part in range(3):
                zcopy(j, j, part).wait_send()
            for axis in range(2):
                for kind in range(4):
                    ring(j, axis, kind).wait_send()


def body(
    train_x,
    train_grad,
    train_routes,
    train_weight,
    train_example,
    probe_x,
    probe_grad,
    probe_routes,
    probe_weight,
    probe_example,
):
    hbm = pl.BlockSpec(memory_space=pl.ANY)
    vmem = pl.BlockSpec(memory_space=pltpu.VMEM)
    dma = pltpu.SemaphoreType.DMA
    return pl.pallas_call(
        kernel,
        out_shape=jax.ShapeDtypeStruct((EX_DEV, LANE), F32),
        in_specs=[hbm, hbm, vmem, vmem, vmem, hbm, hbm, vmem, vmem, vmem],
        out_specs=vmem,
        scratch_shapes=[
            pltpu.VMEM((SLOTS + 1, PANELS, PROW, LANE), BF),
            pltpu.VMEM((2, TOK, D), BF),
            pltpu.VMEM((2, TOP, TOK, KH), BF),
            pltpu.VMEM((4, TOP, TOK, KQ), BF),
            pltpu.VMEM((2, TOP, TOK, KQ), BF),
            pltpu.VMEM((TOP, PROW, KH), BF),
            pltpu.VMEM((6, TOP, TOK, LANE), F32),
            pltpu.VMEM((6, 16, LANE), F32),
            pltpu.VMEM((LANE, LANE), F32),
            pltpu.VMEM((PROW, LANE), F32),
            pltpu.VMEM((PAIRS, 2, TOK, LANE), F32),
            pltpu.VMEM((PAIRS, 2, TOK, LANE), F32),
            pltpu.VMEM((PAIRS, 2, 2, TOK, LANE), BF),
            pltpu.VMEM((PAIRS, 2, 2, TOK, LANE), BF),
            pltpu.VMEM((16, LANE), F32),
            pltpu.VMEM((8, LANE), F32),
            dma((8,)),
            dma((SLOTS, 3)),
            dma((SLOTS, 3)),
            dma((SLOTS, 2, 4)),
            dma((SLOTS, 2, 4)),
            dma((12,)),
            dma((12,)),
            dma((PAIRS, 2)),
            dma((PAIRS, 2)),
        ],
        compiler_params=pltpu.CompilerParams(
            collective_id=0, has_side_effects=True, vmem_limit_bytes=56 * 1024 * 1024
        ),
        cost_estimate=pl.CostEstimate(flops=16_000_000_000, bytes_accessed=6_000_000, transcendentals=0),
        name="ghost_scores",
    )(
        train_x,
        jnp.transpose(train_grad, (1, 0, 2)),
        train_routes.T,
        train_weight.T,
        train_example[None, :],
        probe_x,
        jnp.transpose(probe_grad, (1, 0, 2)),
        probe_routes.T,
        probe_weight.T,
        probe_example[None, :],
    )


def solution(mesh):
    in_specs = (
        P(("dp", "expert"), None),
        P(("dp", "expert"), None, None),
        P(("dp", "expert"), None),
        P(("dp", "expert"), None),
        P(("dp", "expert")),
        P("dp", None),
        P("dp", None, None),
        P("dp", None),
        P("dp", None),
        P("dp"),
    )
    out_specs = P(("dp", "expert"), None)
    return jax.shard_map(body, mesh=mesh, in_specs=in_specs, out_specs=out_specs, check_vma=False)
```

```python
import jax
import jax.numpy as jnp
from jax import lax
from jax.experimental import pallas as pl
from jax.experimental.pallas import tpu as pltpu
from jax.sharding import PartitionSpec as P

MESH = pl.DeviceIdType.MESH
BF = jnp.bfloat16
F32 = jnp.float32

LANE = 128
TOK = 128
PROW = 64
TOP = 6
D = 5120
FF = 1536
NZ = 16
NR = 4
SLOTS = 8
OWN = SLOTS
PEX_ROW = 8
EX_DEV = 4

KQ = FF // 4
KH = FF // 2

XP = D // LANE
GP = KH // LANE
X0 = 1
G0 = X0 + XP
PANELS = G0 + GP * TOP
PARTS = (10, 6)
BASES = (PANELS - NR * PARTS[0], PANELS - NR * sum(PARTS))
PAIRS = 3
UNITS = PAIRS + 2


def nt(a, b):
    return lax.dot_general(a, b, (((1,), (1,)), ((), ())), preferred_element_type=F32)


def split(v):
    hi = v.astype(BF)
    return hi, (v - hi.astype(F32)).astype(BF)


def kernel(
    tx_hbm,
    tg_hbm,
    tr_ref,
    tw_ref,
    te_ref,
    px_hbm,
    pg_hbm,
    pr_ref,
    pw_ref,
    pe_ref,
    out_ref,
    slots,
    tx,
    tg,
    tgx,
    away,
    rawg,
    ids,
    marks,
    square,
    pmarks,
    xs,
    near_sum,
    far_sum,
    back_sum,
    acc,
    rbuf,
    lsem,
    zs,
    zr,
    rs,
    rr,
    es,
    er,
    qs,
    qr,
):
    z = lax.axis_index("dp")
    e = lax.axis_index("expert")
    core = e % 2
    xi = (e // 2) % NR
    yi = e // (2 * NR)
    odd = xi % 2

    def at(zz, xx, yy, cc):
        return (zz, (yy * NR + xx) * 2 + cc)

    xr, xl = (xi + 1) % NR, (xi + NR - 1) % NR
    xp, xn = xi + 1 - 2 * odd, (xi + NR - 1 + 2 * odd) % NR
    yr, yl = (yi + 1) % NR, (yi + NR - 1) % NR
    other = at(z, xi, yi, 1 - core)
    mates = (at(z, xp, yi, core), at(z, xn, yi, core))
    across = (at(z, xp, yi, 1 - core), at(z, xn, yi, 1 - core))
    sides = ((at(z, xi, yr, core), at(z, xi, yl, core)), (at(z, xr, yi, core), at(z, xl, yi, core)))
    ranks = (yi, xi)
    above = at((z + 1) % NZ, xi, yi, core)
    below = at((z + NZ - 1) % NZ, xi, yi, core)
    znext = at((z + NZ - 1 + 2 * core) % NZ, xi, yi, core)
    own = jnp.where(core == 0, OWN, 0)
    first = jnp.where(core == 0, 0, 1)

    barrier = pltpu.get_barrier_semaphore()
    greeted = (other, *mates, *across, *sides[0], above, below)
    for who in greeted:
        pl.semaphore_signal(barrier, inc=1, device_id=who, device_id_type=MESH)

    def quarter(i):
        return pl.ds(pl.multiple_of(i * KQ, LANE), KQ)

    mine = (quarter(odd), quarter(3 - odd))
    theirs = (quarter(1 - odd), quarter(2 + odd))
    parts = (pl.ds(0, KQ), pl.ds(KQ, KQ))
    probe_load = [
        pltpu.make_async_copy(pg_hbm.at[:, :, mine[i]], rawg.at[:, :, parts[i]], lsem.at[i]) for i in range(2)
    ]
    for copy in probe_load:
        copy.start()

    @pl.loop(0, XP)
    def _(c):
        cols = pl.ds(pl.multiple_of(c * LANE, LANE), LANE)
        pltpu.make_async_copy(px_hbm.at[:, cols], slots.at[own, X0 + c], lsem.at[2]).start()

    away_load = [pltpu.make_async_copy(tg_hbm.at[:, :, theirs[i]], away.at[i], lsem.at[3 + i]) for i in range(2)]
    grad_load = [
        pltpu.make_async_copy(tg_hbm.at[:, :, mine[i]], tg.at[0, :, :, parts[i]], lsem.at[5 + i]) for i in range(2)
    ]
    for copy in away_load + grad_load:
        copy.start()
    x_load = pltpu.make_async_copy(tx_hbm, tx.at[0], lsem.at[7])
    x_load.start()

    lane = lax.broadcasted_iota(jnp.int32, (1, LANE), 1)
    square[...] = jnp.zeros_like(square)
    square[0:TOP, 0:PROW] = pr_ref[...].astype(F32)
    square[TOP : TOP + 1, 0:PROW] = pe_ref[...].astype(F32)
    square[8 : 8 + TOP, 0:PROW] = pw_ref[...]
    near = square[0:8, :]
    both = near + pltpu.roll(near, PROW, 1)
    pmarks[...] = jnp.zeros_like(pmarks)
    pmarks[0:TOP, :] = both[0:TOP, :]
    pmarks[TOP : TOP + 1, :] = both[TOP : TOP + 1, :] + (z * PEX_ROW).astype(F32)
    slots[own, 0] = pmarks[...].astype(BF)

    turned = jnp.transpose(square[...])
    for copy in probe_load:
        copy.wait()
    for q in range(TOP):
        scale = jnp.broadcast_to(turned[0:PROW, 8 + q : 9 + q], (PROW, LANE))
        for k in range(GP):
            block = rawg[q, :, k * LANE : (k + 1) * LANE].astype(F32)
            slots[own, G0 + k * TOP + q] = (block * scale).astype(BF)
    pltpu.make_async_copy(slots.at[own, pl.ds(X0, XP)], slots.at[own, pl.ds(X0, XP)], lsem.at[2]).wait()

    def remote(src, dst, send, recv, who):
        return pltpu.make_async_remote_copy(
            src_ref=src, dst_ref=dst, send_sem=send, recv_sem=recv, device_id=who, device_id_type=MESH
        )

    def share(slot, axis, who, begin, count):
        return slots.at[slot, pl.ds(BASES[axis] + PARTS[axis] * who + begin, count)]

    def zcopy(src, dst, part):
        if part < 2:
            pick = lambda slot: share(slot, part, ranks[part], 0, PARTS[part])
        else:
            pick = lambda slot: slots.at[slot, pl.ds(0, BASES[1])]
        return remote(pick(src), pick(dst), zs.at[dst, part], zr.at[dst, part], znext)

    def ring(slot, axis, kind, landing=False):
        size = PARTS[axis]
        who = (0, 0, NR - 1, 1)[kind] + ((NR - 1, 1)[kind % 2] if landing else 0)
        begin, count = ((0, size), (0, size), (0, size // 2), (size // 2, size - size // 2))[kind]
        region = share(slot, axis, (ranks[axis] + who) % NR, begin, count)
        return remote(region, region, rs.at[slot, axis, kind], rr.at[slot, axis, kind], sides[axis][kind % 2])

    pl.semaphore_wait(barrier, len(greeted))
    for part in range(3):
        zcopy(own, first, part).start()

    acc[...] = jnp.zeros_like(acc)
    marks[0] = jnp.zeros((16, LANE), F32)
    marks[0, 0:TOP, :] = tr_ref[...].astype(F32)
    marks[0, TOP : TOP + 1, :] = te_ref[...].astype(F32)
    square[...] = jnp.zeros_like(square)
    square[0:TOP, :] = tr_ref[...].astype(F32)
    square[8 : 8 + TOP, :] = tw_ref[...]
    turned = jnp.transpose(square[...])

    def scale_train(ref, panels):
        for r in range(TOP):
            scale = jnp.broadcast_to(turned[:, 8 + r : 9 + r], (TOK, LANE))

            @pl.loop(0, panels)
            def _(k):
                cols = pl.ds(pl.multiple_of(k * LANE, LANE), LANE)
                ref[r, :, cols] = (ref[r, :, cols].astype(F32) * scale).astype(BF)

    def spread(group):
        square[0:16, :] = marks[group]
        columns = jnp.transpose(square[...])
        for r in range(TOP):
            ids[group, r] = jnp.broadcast_to(columns[:, r : r + 1], (TOK, LANE))

    def swap(src, dst, which, who):
        return remote(src, dst, es.at[which], er.at[which], who)

    swaps = (
        swap(marks.at[0], marks.at[1], 0, other),
        swap(marks.at[0], marks.at[2], 1, mates[0]),
        swap(marks.at[0], marks.at[3], 2, across[0]),
        swap(marks.at[0], marks.at[4], 3, mates[1]),
        swap(marks.at[0], marks.at[5], 4, across[1]),
        swap(away.at[0], tgx.at[0], 5, mates[0]),
        swap(away.at[1], tgx.at[2], 6, mates[1]),
        swap(tx.at[0], tx.at[1], 7, other),
        swap(tg.at[0], tg.at[1], 8, other),
        swap(tgx.at[0], tgx.at[1], 9, other),
        swap(tgx.at[2], tgx.at[3], 10, other),
    )
    for i in range(2):
        away_load[i].wait()
        scale_train(away.at[i], KQ // LANE)
        swaps[5 + i].start()
    for which in range(5):
        swaps[which].start()
    x_load.wait()
    swaps[7].start()
    for copy in grad_load:
        copy.wait()
    scale_train(tg.at[0], GP)
    swaps[8].start()
    spread(0)

    def meet_core():
        swaps[0].wait_recv()
        spread(1)
        swaps[7].wait_recv()
        swaps[8].wait_recv()

    def meet_mates():
        for i in range(2):
            swaps[5 + i].wait_recv()
            swaps[9 + i].start()
        for group in range(2, 6):
            swaps[group - 1].wait_recv()
            spread(group)

    def planes_of(unit, count):
        return [2 * unit, 2 * unit + 1] if count == 2 else [unit + PAIRS]

    def marks_of(unit, count):
        info = [slots[slot, 0, 0:16, :].astype(F32) for slot in planes_of(unit, count)]
        if count == 2:
            info = jnp.where(lane < PROW, info[0], info[1])
            rows = [info[q : q + 1, :] for q in range(TOP)]
        else:
            info = info[0]
            rows = [
                jnp.where(lane < PROW, info[q : q + 1, :], info[q + 1 : q + 2, :]) for q in range(0, TOP, 2)
            ]
        return rows, info[TOP : TOP + 1, :]

    def feature_gram(unit, count):
        planes = planes_of(unit, count)
        px = [jnp.concatenate([slots[slot, X0 + c] for c in range(XP)], axis=1) for slot in planes]
        gram = nt(tx[...].reshape(2 * TOK, D), jnp.concatenate(px * (2 // count), axis=0))
        if count == 1:
            gram = jnp.where(lane < PROW, gram, 0.0)
        xs[unit] = gram.reshape(2, TOK, LANE)

    def route_gram(unit, count, lhs, group, panels):
        rows, _ = marks_of(unit, count)
        planes = planes_of(unit, count)
        pg = jnp.concatenate(
            [
                jnp.concatenate([slots[slot, G0 + k * TOP + q] for q in range(TOP) for slot in planes], axis=0)
                for k in panels
            ],
            axis=1,
        )
        gram = nt(lhs.reshape(TOP * TOK, len(panels) * LANE), pg)
        total = jnp.zeros((TOK, LANE), F32)
        for r in range(TOP):
            who = ids[group, r]
            for q, row in enumerate(rows):
                part = gram[r * TOK : (r + 1) * TOK, q * LANE : (q + 1) * LANE]
                total = total + jnp.where(who == row, part, 0.0)
        if count == 1:
            total = total + pltpu.roll(total, PROW, 1)
        return total

    def give_back(unit, i):
        return remote(far_sum.at[unit, i], back_sum.at[unit, i], qs.at[unit, i], qr.at[unit, i], mates[i])

    def own_tokens(unit, count):
        feature_gram(unit, count)
        for h in range(2):
            near_sum[unit, h] = route_gram(unit, count, tg[h], h, range(GP))

    def mate_tokens(unit, count, i):
        for h in range(2):
            panels = range(i * GP // 2, (i + 1) * GP // 2)
            part = route_gram(unit, count, tgx[2 * i + h], 2 + 2 * i + h, panels)
            far_sum[unit, i, h] = part.astype(BF)
        give_back(unit, i).start()

    def add_scores(units):
        square_rows = lax.broadcasted_iota(jnp.int32, (LANE, LANE), 0).astype(F32)
        rows16 = lax.broadcasted_iota(jnp.int32, (16, TOK), 0).astype(F32)
        owners, values = [], ([], [])
        for unit in units:
            _, owner = marks_of(*((unit, 2) if unit < PAIRS else (unit, 1)))
            owners.append((square_rows == owner).astype(BF))
            for i in range(2):
                give_back(unit, i).wait_recv()
            for h in range(2):
                back = back_sum[unit, 0, h].astype(F32) + back_sum[unit, 1, h].astype(F32)
                values[h].append((near_sum[unit, h] + back) * xs[unit, h])
        owners = jnp.concatenate(owners, axis=1)
        sums = []
        for h in range(2):
            hi, lo = split(jnp.concatenate(values[h], axis=1))
            examples = (rows16 == marks[h, TOP : TOP + 1, :]).astype(BF)
            part = jnp.dot(examples, hi, preferred_element_type=F32)
            part = part + jnp.dot(examples, lo, preferred_element_type=F32)
            sums.append(part[0:8, :])
        hi, lo = split(jnp.concatenate(sums, axis=0))
        acc[...] += nt(hi, owners) + nt(lo, owners)

    def taken(j):
        return (core == 0) | (j >= 1)

    def hop(slot):
        for kind in range(2):
            for axis in range(2):
                ring(slot, axis, kind, True).wait_recv()
                ring(slot, axis, kind + 2).start()

    def filled(slot):
        for kind in range(2, 4):
            for axis in range(2):
                ring(slot, axis, kind, True).wait_recv()

    @pl.loop(0, SLOTS)
    def _(j):
        home = (j >= 3) & (j % 2 == 1)
        pair = jnp.clip((j - 3) // 2, 0, PAIRS - 1)
        visit = ((j >= 4) & (j % 2 == 0)) | (j == SLOTS - 1)

        def pass_on(part):
            @pl.when(taken(j))
            def _():
                zcopy(j, j, part).wait_recv()

                @pl.when(j < SLOTS - 1)
                def _():
                    zcopy(j, jnp.minimum(j + 1, SLOTS - 1), part).start()

                if part < 2:
                    ring(j, part, 0).start()
                    ring(j, part, 1).start()

        pass_on(0)
        pass_on(1)
        pl.when((j >= 1) & taken(j - 1))(lambda: hop(jnp.maximum(j - 1, 0)))
        pl.when((j >= 2) & taken(j - 2))(lambda: filled(jnp.maximum(j - 2, 0)))

        @pl.when(j == 4)
        def _():
            swaps[9].wait_recv()
            swaps[10].wait_recv()

        pl.when(home)(lambda: own_tokens(pair, 2))
        pl.when(visit)(lambda: mate_tokens(pair, 2, 0))
        pass_on(2)
        pl.when(visit)(lambda: mate_tokens(pair, 2, 1))
        pl.when(j == 2)(meet_core)
        pl.when(j == 3)(meet_mates)

    @pl.loop(PAIRS, UNITS)
    def _(unit):
        filled(unit + PAIRS)
        mate_tokens(unit, 1, 0)
        pl.when(unit == PAIRS)(lambda: hop(SLOTS - 1))
        mate_tokens(unit, 1, 1)
        own_tokens(unit, 1)
        pl.when(unit == PAIRS)(lambda: add_scores(range(PAIRS + 1)))

    add_scores([UNITS - 1])

    last = swap(acc.at[pl.ds(8, 8)], rbuf, 11, other)
    last.start()
    last.wait_recv()
    out_ref[...] = acc[0:EX_DEV, :] + rbuf[0:EX_DEV, :]

    last.wait_send()
    for copy in swaps:
        copy.wait_send()

    @pl.loop(0, UNITS)
    def _(unit):
        for i in range(2):
            give_back(unit, i).wait_send()

    @pl.loop(0, SLOTS)
    def _(j):
        @pl.when(taken(j))
        def _():
            for part in range(3):
                zcopy(j, j, part).wait_send()
            for axis in range(2):
                for kind in range(4):
                    ring(j, axis, kind).wait_send()


def body(
    train_x,
    train_grad,
    train_routes,
    train_weight,
    train_example,
    probe_x,
    probe_grad,
    probe_routes,
    probe_weight,
    probe_example,
):
    hbm = pl.BlockSpec(memory_space=pl.ANY)
    vmem = pl.BlockSpec(memory_space=pltpu.VMEM)
    dma = pltpu.SemaphoreType.DMA
    return pl.pallas_call(
        kernel,
        out_shape=jax.ShapeDtypeStruct((EX_DEV, LANE), F32),
        in_specs=[hbm, hbm, vmem, vmem, vmem, hbm, hbm, vmem, vmem, vmem],
        out_specs=vmem,
        scratch_shapes=[
            pltpu.VMEM((SLOTS + 1, PANELS, PROW, LANE), BF),
            pltpu.VMEM((2, TOK, D), BF),
            pltpu.VMEM((2, TOP, TOK, KH), BF),
            pltpu.VMEM((4, TOP, TOK, KQ), BF),
            pltpu.VMEM((2, TOP, TOK, KQ), BF),
            pltpu.VMEM((TOP, PROW, KH), BF),
            pltpu.VMEM((6, TOP, TOK, LANE), F32),
            pltpu.VMEM((6, 16, LANE), F32),
            pltpu.VMEM((LANE, LANE), F32),
            pltpu.VMEM((PROW, LANE), F32),
            pltpu.VMEM((UNITS, 2, TOK, LANE), F32),
            pltpu.VMEM((UNITS, 2, TOK, LANE), F32),
            pltpu.VMEM((UNITS, 2, 2, TOK, LANE), BF),
            pltpu.VMEM((UNITS, 2, 2, TOK, LANE), BF),
            pltpu.VMEM((16, LANE), F32),
            pltpu.VMEM((8, LANE), F32),
            dma((8,)),
            dma((SLOTS, 3)),
            dma((SLOTS, 3)),
            dma((SLOTS, 2, 4)),
            dma((SLOTS, 2, 4)),
            dma((12,)),
            dma((12,)),
            dma((UNITS, 2)),
            dma((UNITS, 2)),
        ],
        compiler_params=pltpu.CompilerParams(
            collective_id=0, has_side_effects=True, vmem_limit_bytes=56 * 1024 * 1024
        ),
        cost_estimate=pl.CostEstimate(flops=16_000_000_000, bytes_accessed=6_000_000, transcendentals=0),
        name="ghost_scores",
    )(
        train_x,
        jnp.transpose(train_grad, (1, 0, 2)),
        train_routes.T,
        train_weight.T,
        train_example[None, :],
        probe_x,
        jnp.transpose(probe_grad, (1, 0, 2)),
        probe_routes.T,
        probe_weight.T,
        probe_example[None, :],
    )


def solution(mesh):
    in_specs = (
        P(("dp", "expert"), None),
        P(("dp", "expert"), None, None),
        P(("dp", "expert"), None),
        P(("dp", "expert"), None),
        P(("dp", "expert")),
        P("dp", None),
        P("dp", None, None),
        P("dp", None),
        P("dp", None),
        P("dp"),
    )
    out_specs = P(("dp", "expert"), None)
    return jax.shard_map(body, mesh=mesh, in_specs=in_specs, out_specs=out_specs, check_vma=False)
```

```python
import jax
import jax.numpy as jnp
from jax import lax
from jax.experimental import pallas as pl
from jax.experimental.pallas import tpu as pltpu
from jax.sharding import PartitionSpec as P

MESH = pl.DeviceIdType.MESH
BF = jnp.bfloat16
F32 = jnp.float32

LANE = 128
TOK = 128
PROW = 64
TOP = 6
D = 5120
FF = 1536
NZ = 16
NR = 4
SLOTS = 8
OWN = SLOTS
PEX_ROW = 8
EX_DEV = 4

KQ = FF // 4
KH = FF // 2

XP = D // LANE
GP = KH // LANE
X0 = 1
G0 = X0 + XP
PANELS = G0 + GP * TOP
PARTS = (10, 6)
BASES = (PANELS - NR * PARTS[0], PANELS - NR * sum(PARTS))
LAG = 2
MEET = 4


def nt(a, b):
    return lax.dot_general(a, b, (((1,), (1,)), ((), ())), preferred_element_type=F32)


def split(v):
    hi = v.astype(BF)
    return hi, (v - hi.astype(F32)).astype(BF)


def kernel(
    tx_hbm,
    tg_hbm,
    tr_ref,
    tw_ref,
    te_ref,
    px_hbm,
    pg_hbm,
    pr_ref,
    pw_ref,
    pe_ref,
    out_ref,
    slots,
    tx,
    tg,
    tgx,
    away,
    rawx,
    rawt,
    rawa,
    rawg,
    marks,
    square,
    xs,
    near_sum,
    far_sum,
    back_sum,
    acc,
    rbuf,
    lsem,
    zs,
    zr,
    rs,
    rr,
    es,
    er,
    qs,
    qr,
):
    z = lax.axis_index("dp")
    e = lax.axis_index("expert")
    core = e % 2
    xi = (e // 2) % NR
    yi = e // (2 * NR)
    odd = xi % 2

    def at(zz, xx, yy, cc):
        return (zz, (yy * NR + xx) * 2 + cc)

    xr, xl = (xi + 1) % NR, (xi + NR - 1) % NR
    xp, xn = xi + 1 - 2 * odd, (xi + NR - 1 + 2 * odd) % NR
    yr, yl = (yi + 1) % NR, (yi + NR - 1) % NR
    other = at(z, xi, yi, 1 - core)
    mates = (at(z, xp, yi, core), at(z, xn, yi, core))
    across = (at(z, xp, yi, 1 - core), at(z, xn, yi, 1 - core))
    sides = ((at(z, xi, yr, core), at(z, xi, yl, core)), (at(z, xr, yi, core), at(z, xl, yi, core)))
    ranks = (yi, xi)
    above = at((z + 1) % NZ, xi, yi, core)
    below = at((z + NZ - 1) % NZ, xi, yi, core)
    znext = at((z + NZ - 1 + 2 * core) % NZ, xi, yi, core)
    own = jnp.where(core == 0, OWN, 0)
    first = jnp.where(core == 0, 0, 1)

    barrier = pltpu.get_barrier_semaphore()
    greeted = (other, *mates, *across, *sides[0], above, below)
    for who in greeted:
        pl.semaphore_signal(barrier, inc=1, device_id=who, device_id_type=MESH)

    def quarter(i):
        return pl.ds(pl.multiple_of(i * KQ, LANE), KQ)

    mine = (quarter(odd), quarter(3 - odd))
    theirs = (quarter(1 - odd), quarter(2 + odd))
    parts = (pl.ds(0, KQ), pl.ds(KQ, KQ))
    probe_load = [
        pltpu.make_async_copy(pg_hbm.at[:, :, mine[i]], rawg.at[:, :, parts[i]], lsem.at[i]) for i in range(2)
    ]
    for copy in probe_load:
        copy.start()

    @pl.loop(0, XP)
    def _(c):
        cols = pl.ds(pl.multiple_of(c * LANE, LANE), LANE)
        pltpu.make_async_copy(px_hbm.at[:, cols], slots.at[own, X0 + c], lsem.at[2]).start()

    away_load = [pltpu.make_async_copy(tg_hbm.at[:, :, theirs[i]], rawa.at[i], lsem.at[3 + i]) for i in range(2)]
    grad_load = [
        pltpu.make_async_copy(tg_hbm.at[:, :, mine[i]], rawt.at[:, :, parts[i]], lsem.at[5 + i]) for i in range(2)
    ]
    for copy in away_load + grad_load:
        copy.start()
    x_load = pltpu.make_async_copy(tx_hbm, rawx, lsem.at[7])
    x_load.start()

    lane = lax.broadcasted_iota(jnp.int32, (1, LANE), 1)
    square[...] = jnp.zeros_like(square)
    square[0:TOP, 0:PROW] = pr_ref[...].astype(F32)
    square[TOP : TOP + 1, 0:PROW] = pe_ref[...].astype(F32) + (z * PEX_ROW).astype(F32)
    square[8 : 8 + TOP, 0:PROW] = pw_ref[...]
    turned = jnp.transpose(square[...])
    slots[own, 0] = jnp.where(lane <= TOP, turned[0:PROW, :], 0.0).astype(BF)

    for copy in probe_load:
        copy.wait()
    for q in range(TOP):
        scale = jnp.broadcast_to(turned[0:PROW, 8 + q : 9 + q], (PROW, LANE))
        for k in range(GP):
            block = rawg[q, :, k * LANE : (k + 1) * LANE].astype(F32)
            slots[own, G0 + k * TOP + q] = (block * scale).astype(BF)
    pltpu.make_async_copy(slots.at[own, pl.ds(X0, XP)], slots.at[own, pl.ds(X0, XP)], lsem.at[2]).wait()

    def remote(src, dst, send, recv, who):
        return pltpu.make_async_remote_copy(
            src_ref=src, dst_ref=dst, send_sem=send, recv_sem=recv, device_id=who, device_id_type=MESH
        )

    def share(slot, axis, who, begin, count):
        return slots.at[slot, pl.ds(BASES[axis] + PARTS[axis] * who + begin, count)]

    def zcopy(src, dst, part):
        if part < 2:
            pick = lambda slot: share(slot, part, ranks[part], 0, PARTS[part])
        else:
            pick = lambda slot: slots.at[slot, pl.ds(0, BASES[1])]
        return remote(pick(src), pick(dst), zs.at[dst, part], zr.at[dst, part], znext)

    def ring(slot, axis, kind, landing=False):
        size = PARTS[axis]
        who = (0, 0, NR - 1, 1)[kind] + ((NR - 1, 1)[kind % 2] if landing else 0)
        begin, count = ((0, size), (0, size), (0, size // 2), (size // 2, size - size // 2))[kind]
        region = share(slot, axis, (ranks[axis] + who) % NR, begin, count)
        return remote(region, region, rs.at[slot, axis, kind], rr.at[slot, axis, kind], sides[axis][kind % 2])

    pl.semaphore_wait(barrier, len(greeted))
    for part in range(3):
        zcopy(own, first, part).start()

    acc[...] = jnp.zeros_like(acc)
    marks[0] = jnp.zeros((16, LANE), F32)
    marks[0, 0:TOP, :] = tr_ref[...].astype(F32)
    marks[0, TOP : TOP + 1, :] = te_ref[...].astype(F32)
    square[...] = jnp.zeros_like(square)
    square[0:TOP, :] = tw_ref[...]

    def turn_grad(src, dst, panels):
        weights = jnp.transpose(square[...])
        for r in range(TOP):
            scale = jnp.broadcast_to(weights[:, r : r + 1], (TOK, LANE))

            @pl.loop(0, panels)
            def _(k):
                cols = pl.ds(pl.multiple_of(k * LANE, LANE), LANE)
                block = (src[r, :, cols].astype(F32) * scale).astype(BF).astype(F32)
                dst[cols, r * TOK : (r + 1) * TOK] = jnp.transpose(block).astype(BF)

    def turn_x():
        @pl.loop(0, XP)
        def _(k):
            cols = pl.ds(pl.multiple_of(k * LANE, LANE), LANE)
            tx[0, cols, :] = jnp.transpose(rawx[:, cols].astype(F32)).astype(BF)

    def swap(src, dst, which, who):
        return remote(src, dst, es.at[which], er.at[which], who)

    swaps = (
        swap(marks.at[0], marks.at[1], 0, other),
        swap(marks.at[0], marks.at[2], 1, mates[0]),
        swap(marks.at[0], marks.at[3], 2, across[0]),
        swap(marks.at[0], marks.at[4], 3, mates[1]),
        swap(marks.at[0], marks.at[5], 4, across[1]),
        swap(away.at[0], tgx.at[0], 5, mates[0]),
        swap(away.at[1], tgx.at[2], 6, mates[1]),
        swap(tx.at[0], tx.at[1], 7, other),
        swap(tg.at[0], tg.at[1], 8, other),
        swap(tgx.at[0], tgx.at[1], 9, other),
        swap(tgx.at[2], tgx.at[3], 10, other),
    )
    for i in range(2):
        away_load[i].wait()
        turn_grad(rawa.at[i], away.at[i], KQ // LANE)
        swaps[5 + i].start()
    for which in range(5):
        swaps[which].start()

    def give_core_grad():
        for copy in grad_load:
            copy.wait()
        turn_grad(rawt, tg.at[0], GP)
        swaps[8].start()

    def give_core_x():
        x_load.wait()
        turn_x()
        swaps[7].start()

    def meet_core():
        swaps[0].wait_recv()
        swaps[7].wait_recv()
        swaps[8].wait_recv()

    def meet_mates():
        for i in range(2):
            swaps[5 + i].wait_recv()
            swaps[9 + i].start()
        for which in range(1, 5):
            swaps[which].wait_recv()

    def feature_gram(slot):
        px = jnp.concatenate([slots[slot, X0 + c] for c in range(XP)], axis=1)
        gram = jnp.dot(px, jnp.concatenate([tx[0], tx[1]], axis=1), preferred_element_type=F32)
        for h in range(2):
            xs[slot, h] = gram[:, h * TOK : (h + 1) * TOK]

    def route_gram(slot, rhs, group, panels):
        info = slots[slot, 0].astype(F32)
        pg = jnp.concatenate(
            [slots[slot, G0 + k * TOP : G0 + (k + 1) * TOP].reshape(TOP * PROW, LANE) for k in panels], axis=1
        )
        gram = jnp.dot(pg, rhs, preferred_element_type=F32)
        total = jnp.zeros((PROW, LANE), F32)
        for q in range(TOP):
            who = jnp.broadcast_to(info[:, q : q + 1], (PROW, LANE))
            for r in range(TOP):
                part = gram[q * PROW : (q + 1) * PROW, r * TOK : (r + 1) * TOK]
                total = total + jnp.where(who == marks[group, r : r + 1, :], part, 0.0)
        return total

    def give_back(slot, i):
        return remote(far_sum.at[slot, i], back_sum.at[slot, i], qs.at[slot, i], qr.at[slot, i], mates[i])

    def own_tokens(slot):
        feature_gram(slot)
        for h in range(2):
            near_sum[slot, h] = route_gram(slot, tg[h], h, range(GP))

    def mate_tokens(slot):
        for i in range(2):
            panels = range(i * GP // 2, (i + 1) * GP // 2)
            for h in range(2):
                far_sum[slot, i, h] = route_gram(slot, tgx[2 * i + h], 2 + 2 * i + h, panels).astype(BF)
            give_back(slot, i).start()

    def add_scores(some):
        rows16 = lax.broadcasted_iota(jnp.int32, (16, TOK), 0).astype(F32)
        classes = lane.astype(F32)
        owners, values = [], ([], [])
        for slot in some:
            owners.append((slots[slot, 0].astype(F32)[:, TOP : TOP + 1] == classes).astype(BF))
            for i in range(2):
                give_back(slot, i).wait_recv()
            for h in range(2):
                back = back_sum[slot, 0, h].astype(F32) + back_sum[slot, 1, h].astype(F32)
                values[h].append((near_sum[slot, h] + back) * xs[slot, h])
        owners = jnp.concatenate(owners, axis=0)
        sums = []
        for h in range(2):
            hi, lo = split(jnp.concatenate(values[h], axis=0))
            examples = (rows16 == marks[h, TOP : TOP + 1, :]).astype(BF)
            sums.append((nt(examples, hi) + nt(examples, lo))[0:8, :])
        hi, lo = split(jnp.concatenate(sums, axis=0))
        part = jnp.dot(hi, owners, preferred_element_type=F32)
        acc[...] += part + jnp.dot(lo, owners, preferred_element_type=F32)

    def taken(j):
        return (core == 0) | (j >= 1)

    @pl.loop(0, SLOTS + LAG)
    def _(j):
        fresh = (j < SLOTS) & taken(j)

        def pass_on(part):
            @pl.when(fresh)
            def _():
                zcopy(j, j, part).wait_recv()

                @pl.when(j < SLOTS - 1)
                def _():
                    zcopy(j, jnp.minimum(j + 1, SLOTS - 1), part).start()

                if part < 2:
                    ring(j, part, 0).start()
                    ring(j, part, 1).start()

        pass_on(0)
        pass_on(1)

        @pl.when((j >= 1) & (j < SLOTS + 1) & taken(j - 1))
        def _():
            slot = jnp.maximum(j - 1, 0)
            for kind in range(2):
                for axis in range(2):
                    ring(slot, axis, kind, True).wait_recv()
                    ring(slot, axis, kind + 2).start()

        pl.when(j == 0)(give_core_grad)
        pl.when(j == 1)(give_core_x)
        pl.when(j == LAG)(meet_core)
        pl.when(j == SLOTS + LAG - 1)(lambda: add_scores(range(SLOTS - 1)))

        @pl.when((j >= 2) & (j < SLOTS + 2) & taken(j - 2))
        def _():
            slot = jnp.maximum(j - 2, 0)
            for kind in range(2, 4):
                for axis in range(2):
                    ring(slot, axis, kind, True).wait_recv()

        @pl.when(j >= MEET)
        def _():
            @pl.when(j == MEET)
            def _():
                swaps[9].wait_recv()
                swaps[10].wait_recv()

            late = 2 * (j - MEET)
            begin = jnp.minimum(late, j - LAG)
            end = jnp.minimum(late + 2, j - LAG + 1)
            pl.loop(begin, end)(mate_tokens)

        pass_on(2)
        pl.when(j >= LAG)(lambda: own_tokens(jnp.maximum(j - LAG, 0)))
        pl.when(j == MEET - 1)(meet_mates)

    add_scores([SLOTS - 1])

    last = swap(acc.at[pl.ds(8, 8)], rbuf, 11, other)
    last.start()
    last.wait_recv()
    out_ref[...] = acc[0:EX_DEV, :] + rbuf[0:EX_DEV, :]

    last.wait_send()
    for copy in swaps:
        copy.wait_send()

    @pl.loop(0, SLOTS)
    def _(slot):
        for i in range(2):
            give_back(slot, i).wait_send()

    @pl.loop(0, SLOTS)
    def _(j):
        @pl.when(taken(j))
        def _():
            for part in range(3):
                zcopy(j, j, part).wait_send()
            for axis in range(2):
                for kind in range(4):
                    ring(j, axis, kind).wait_send()


def body(
    train_x,
    train_grad,
    train_routes,
    train_weight,
    train_example,
    probe_x,
    probe_grad,
    probe_routes,
    probe_weight,
    probe_example,
):
    hbm = pl.BlockSpec(memory_space=pl.ANY)
    vmem = pl.BlockSpec(memory_space=pltpu.VMEM)
    dma = pltpu.SemaphoreType.DMA
    return pl.pallas_call(
        kernel,
        out_shape=jax.ShapeDtypeStruct((EX_DEV, LANE), F32),
        in_specs=[hbm, hbm, vmem, vmem, vmem, hbm, hbm, vmem, vmem, vmem],
        out_specs=vmem,
        scratch_shapes=[
            pltpu.VMEM((SLOTS + 1, PANELS, PROW, LANE), BF),
            pltpu.VMEM((2, D, TOK), BF),
            pltpu.VMEM((2, KH, TOP * TOK), BF),
            pltpu.VMEM((4, KQ, TOP * TOK), BF),
            pltpu.VMEM((2, KQ, TOP * TOK), BF),
            pltpu.VMEM((TOK, D), BF),
            pltpu.VMEM((TOP, TOK, KH), BF),
            pltpu.VMEM((2, TOP, TOK, KQ), BF),
            pltpu.VMEM((TOP, PROW, KH), BF),
            pltpu.VMEM((6, 16, LANE), F32),
            pltpu.VMEM((LANE, LANE), F32),
            pltpu.VMEM((SLOTS, 2, PROW, LANE), F32),
            pltpu.VMEM((SLOTS, 2, PROW, LANE), F32),
            pltpu.VMEM((SLOTS, 2, 2, PROW, LANE), BF),
            pltpu.VMEM((SLOTS, 2, 2, PROW, LANE), BF),
            pltpu.VMEM((16, LANE), F32),
            pltpu.VMEM((8, LANE), F32),
            dma((8,)),
            dma((SLOTS, 3)),
            dma((SLOTS, 3)),
            dma((SLOTS, 2, 4)),
            dma((SLOTS, 2, 4)),
            dma((12,)),
            dma((12,)),
            dma((SLOTS, 2)),
            dma((SLOTS, 2)),
        ],
        compiler_params=pltpu.CompilerParams(
            collective_id=0, has_side_effects=True, vmem_limit_bytes=56 * 1024 * 1024
        ),
        cost_estimate=pl.CostEstimate(flops=16_000_000_000, bytes_accessed=6_000_000, transcendentals=0),
        name="ghost_scores",
    )(
        train_x,
        jnp.transpose(train_grad, (1, 0, 2)),
        train_routes.T,
        train_weight.T,
        train_example[None, :],
        probe_x,
        jnp.transpose(probe_grad, (1, 0, 2)),
        probe_routes.T,
        probe_weight.T,
        probe_example[None, :],
    )


def solution(mesh):
    in_specs = (
        P(("dp", "expert"), None),
        P(("dp", "expert"), None, None),
        P(("dp", "expert"), None),
        P(("dp", "expert"), None),
        P(("dp", "expert")),
        P("dp", None),
        P("dp", None, None),
        P("dp", None),
        P("dp", None),
        P("dp"),
    )
    out_specs = P(("dp", "expert"), None)
    return jax.shard_map(body, mesh=mesh, in_specs=in_specs, out_specs=out_specs, check_vma=False)
```

```python
import jax
import jax.numpy as jnp
from jax import lax
from jax.experimental import pallas as pl
from jax.experimental.pallas import tpu as pltpu
from jax.sharding import PartitionSpec as P

MESH = pl.DeviceIdType.MESH
BF = jnp.bfloat16
F32 = jnp.float32

LANE = 128
TOK = 128
PROW = 64
TOP = 6
D = 5120
FF = 1536
NZ = 16
NR = 4
SLOTS = 8
OWN = SLOTS
PEX_ROW = 8
EX_DEV = 4

KQ = FF // 4
KH = FF // 2

XP = D // LANE
GP = KH // LANE
X0 = 1
G0 = X0 + XP
PANELS = G0 + GP * TOP
PARTS = (10, 6)
BASES = (PANELS - NR * PARTS[0], PANELS - NR * sum(PARTS))
PAIRS = SLOTS // 2


def nt(a, b):
    return lax.dot_general(a, b, (((1,), (1,)), ((), ())), preferred_element_type=F32)


def split(v):
    hi = v.astype(BF)
    return hi, (v - hi.astype(F32)).astype(BF)


def kernel(
    tx_hbm,
    tg_hbm,
    tr_ref,
    tw_ref,
    te_ref,
    px_hbm,
    pg_hbm,
    pr_ref,
    pw_ref,
    pe_ref,
    out_ref,
    slots,
    tx,
    tg,
    tgx,
    away,
    rawg,
    ids,
    marks,
    square,
    pmarks,
    xs,
    near_sum,
    far_sum,
    back_sum,
    acc,
    rbuf,
    lsem,
    zs,
    zr,
    rs,
    rr,
    es,
    er,
    qs,
    qr,
):
    z = lax.axis_index("dp")
    e = lax.axis_index("expert")
    core = e % 2
    xi = (e // 2) % NR
    yi = e // (2 * NR)
    odd = xi % 2

    def at(zz, xx, yy, cc):
        return (zz, (yy * NR + xx) * 2 + cc)

    xr, xl = (xi + 1) % NR, (xi + NR - 1) % NR
    xp, xn = xi + 1 - 2 * odd, (xi + NR - 1 + 2 * odd) % NR
    yr, yl = (yi + 1) % NR, (yi + NR - 1) % NR
    other = at(z, xi, yi, 1 - core)
    mates = (at(z, xp, yi, core), at(z, xn, yi, core))
    across = (at(z, xp, yi, 1 - core), at(z, xn, yi, 1 - core))
    sides = ((at(z, xi, yr, core), at(z, xi, yl, core)), (at(z, xr, yi, core), at(z, xl, yi, core)))
    ranks = (yi, xi)
    above = at((z + 1) % NZ, xi, yi, core)
    below = at((z + NZ - 1) % NZ, xi, yi, core)
    znext = at((z + NZ - 1 + 2 * core) % NZ, xi, yi, core)
    own = jnp.where(core == 0, OWN, 0)
    first = jnp.where(core == 0, 0, 1)

    barrier = pltpu.get_barrier_semaphore()
    greeted = (other, *mates, *across, *sides[0], above, below)
    for who in greeted:
        pl.semaphore_signal(barrier, inc=1, device_id=who, device_id_type=MESH)

    def quarter(i):
        return pl.ds(pl.multiple_of(i * KQ, LANE), KQ)

    mine = (quarter(odd), quarter(3 - odd))
    theirs = (quarter(1 - odd), quarter(2 + odd))
    parts = (pl.ds(0, KQ), pl.ds(KQ, KQ))
    probe_load = [
        pltpu.make_async_copy(pg_hbm.at[:, :, mine[i]], rawg.at[:, :, parts[i]], lsem.at[i]) for i in range(2)
    ]
    for copy in probe_load:
        copy.start()

    @pl.loop(0, XP)
    def _(c):
        cols = pl.ds(pl.multiple_of(c * LANE, LANE), LANE)
        pltpu.make_async_copy(px_hbm.at[:, cols], slots.at[own, X0 + c], lsem.at[2]).start()

    away_load = [pltpu.make_async_copy(tg_hbm.at[:, :, theirs[i]], away.at[i], lsem.at[3 + i]) for i in range(2)]
    grad_load = [
        pltpu.make_async_copy(tg_hbm.at[:, :, mine[i]], tg.at[0, :, :, parts[i]], lsem.at[5 + i]) for i in range(2)
    ]
    for copy in away_load + grad_load:
        copy.start()
    x_load = pltpu.make_async_copy(tx_hbm, tx.at[0], lsem.at[7])
    x_load.start()

    lane = lax.broadcasted_iota(jnp.int32, (1, LANE), 1)
    square[...] = jnp.zeros_like(square)
    square[0:TOP, 0:PROW] = pr_ref[...].astype(F32)
    square[TOP : TOP + 1, 0:PROW] = pe_ref[...].astype(F32)
    square[8 : 8 + TOP, 0:PROW] = pw_ref[...]
    near = square[0:8, :]
    both = near + pltpu.roll(near, PROW, 1)
    pmarks[...] = jnp.zeros_like(pmarks)
    pmarks[0:TOP, :] = both[0:TOP, :]
    pmarks[TOP : TOP + 1, :] = both[TOP : TOP + 1, :] + (z * PEX_ROW).astype(F32)
    slots[own, 0] = pmarks[...].astype(BF)

    turned = jnp.transpose(square[...])
    for copy in probe_load:
        copy.wait()
    for q in range(TOP):
        scale = jnp.broadcast_to(turned[0:PROW, 8 + q : 9 + q], (PROW, LANE))
        for k in range(GP):
            block = rawg[q, :, k * LANE : (k + 1) * LANE].astype(F32)
            slots[own, G0 + k * TOP + q] = (block * scale).astype(BF)
    pltpu.make_async_copy(slots.at[own, pl.ds(X0, XP)], slots.at[own, pl.ds(X0, XP)], lsem.at[2]).wait()

    def remote(src, dst, send, recv, who):
        return pltpu.make_async_remote_copy(
            src_ref=src, dst_ref=dst, send_sem=send, recv_sem=recv, device_id=who, device_id_type=MESH
        )

    def share(slot, axis, who, begin, count):
        return slots.at[slot, pl.ds(BASES[axis] + PARTS[axis] * who + begin, count)]

    def zcopy(src, dst, part):
        if part < 2:
            pick = lambda slot: share(slot, part, ranks[part], 0, PARTS[part])
        else:
            pick = lambda slot: slots.at[slot, pl.ds(0, BASES[1])]
        return remote(pick(src), pick(dst), zs.at[dst, part], zr.at[dst, part], znext)

    def ring(slot, axis, kind, landing=False):
        size = PARTS[axis]
        who = (0, 0, NR - 1, 1)[kind] + ((NR - 1, 1)[kind % 2] if landing else 0)
        begin, count = ((0, size), (0, size), (0, size // 2), (size // 2, size - size // 2))[kind]
        region = share(slot, axis, (ranks[axis] + who) % NR, begin, count)
        return remote(region, region, rs.at[slot, axis, kind], rr.at[slot, axis, kind], sides[axis][kind % 2])

    pl.semaphore_wait(barrier, len(greeted))
    for part in range(3):
        zcopy(own, first, part).start()

    marks[0] = jnp.zeros((16, LANE), F32)
    marks[0, 0:TOP, :] = tr_ref[...].astype(F32)
    marks[0, TOP : TOP + 1, :] = te_ref[...].astype(F32)
    square[...] = jnp.zeros_like(square)
    square[0:TOP, :] = tr_ref[...].astype(F32)
    square[8 : 8 + TOP, :] = tw_ref[...]
    turned = jnp.transpose(square[...])

    def scale_train(ref, panels):
        for r in range(TOP):
            scale = jnp.broadcast_to(turned[:, 8 + r : 9 + r], (TOK, LANE))

            @pl.loop(0, panels)
            def _(k):
                cols = pl.ds(pl.multiple_of(k * LANE, LANE), LANE)
                ref[r, :, cols] = (ref[r, :, cols].astype(F32) * scale).astype(BF)

    def spread(group):
        square[0:16, :] = marks[group]
        columns = jnp.transpose(square[...])
        for r in range(TOP):
            ids[group, r] = jnp.broadcast_to(columns[:, r : r + 1], (TOK, LANE))

    def swap(src, dst, which, who):
        return remote(src, dst, es.at[which], er.at[which], who)

    swaps = (
        swap(marks.at[0], marks.at[1], 0, other),
        swap(marks.at[0], marks.at[2], 1, mates[0]),
        swap(marks.at[0], marks.at[3], 2, across[0]),
        swap(marks.at[0], marks.at[4], 3, mates[1]),
        swap(marks.at[0], marks.at[5], 4, across[1]),
        swap(away.at[0], tgx.at[0], 5, mates[0]),
        swap(away.at[1], tgx.at[2], 6, mates[1]),
        swap(tx.at[0], tx.at[1], 7, other),
        swap(tg.at[0], tg.at[1], 8, other),
        swap(tgx.at[0], tgx.at[1], 9, other),
        swap(tgx.at[2], tgx.at[3], 10, other),
    )
    for i in range(2):
        away_load[i].wait()
        scale_train(away.at[i], KQ // LANE)
        swaps[5 + i].start()
    for which in range(5):
        swaps[which].start()
    x_load.wait()
    swaps[7].start()
    for copy in grad_load:
        copy.wait()
    scale_train(tg.at[0], GP)
    swaps[8].start()
    spread(0)

    def meet_core():
        swaps[0].wait_recv()
        spread(1)
        swaps[7].wait_recv()
        swaps[8].wait_recv()

    def meet_mates():
        for i in range(2):
            swaps[5 + i].wait_recv()
            swaps[9 + i].start()
        for group in range(2, 6):
            swaps[group - 1].wait_recv()
            spread(group)

    def feature_gram(pair):
        px = [jnp.concatenate([slots[2 * pair - 2 + i, X0 + c] for c in range(XP)], axis=1) for i in range(4)]
        gram = nt(tx[...].reshape(2 * TOK, D), jnp.concatenate(px, axis=0))
        for i in range(2):
            for h in range(2):
                xs[pair - 1 + i, h] = gram[h * TOK : (h + 1) * TOK, i * LANE : (i + 1) * LANE]

    def route_gram(pair, lhs, group, panels):
        info = [slots[2 * pair + i, 0, 0:16, :].astype(F32) for i in range(2)]
        info = jnp.where(lane < PROW, info[0], info[1])
        pg = jnp.concatenate(
            [
                jnp.concatenate(
                    [slots[2 * pair + i, G0 + k * TOP + q] for q in range(TOP) for i in range(2)], axis=0
                )
                for k in panels
            ],
            axis=1,
        )
        gram = nt(lhs.reshape(2 * TOP * TOK, len(panels) * LANE), pg)
        sums = []
        for h in range(2):
            total = jnp.zeros((TOK, LANE), F32)
            for r in range(TOP):
                who = ids[group + h, r]
                row = (h * TOP + r) * TOK
                for q in range(TOP):
                    part = gram[row : row + TOK, q * LANE : (q + 1) * LANE]
                    total = total + jnp.where(who == info[q : q + 1, :], part, 0.0)
            sums.append(total)
        return sums

    def give_back(pair, i):
        return remote(far_sum.at[pair, i], back_sum.at[pair, i], qs.at[pair, i], qr.at[pair, i], mates[i])

    def own_tokens(pair):
        for h, total in enumerate(route_gram(pair, tg[...], 0, range(GP))):
            near_sum[pair, h] = total

    def mate_tokens(pair, i):
        panels = range(i * GP // 2, (i + 1) * GP // 2)
        for h, total in enumerate(route_gram(pair, tgx[2 * i : 2 * i + 2], 2 + 2 * i, panels)):
            far_sum[pair, i, h] = total.astype(BF)
        give_back(pair, i).start()

    def taken(j):
        return (core == 0) | (j >= 1)

    @pl.loop(0, SLOTS + 3)
    def _(j):
        odd_step = j % 2 == 1
        home = ((j >= 3) & (j < SLOTS) & odd_step) | (j == SLOTS + 2)
        visit = ((j >= 4) & (j <= SLOTS) & ~odd_step) | (j == SLOTS + 1)
        pair = jnp.clip((j - 3) // 2, 0, PAIRS - 1)

        def pass_on(part):
            @pl.when((j < SLOTS) & taken(j))
            def _():
                zcopy(j, j, part).wait_recv()

                @pl.when(j < SLOTS - 1)
                def _():
                    zcopy(j, jnp.minimum(j + 1, SLOTS - 1), part).start()

                if part < 2:
                    ring(j, part, 0).start()
                    ring(j, part, 1).start()

        pass_on(0)
        pass_on(1)

        @pl.when((j >= 1) & (j < SLOTS + 1) & taken(j - 1))
        def _():
            slot = jnp.clip(j - 1, 0, SLOTS - 1)
            for kind in range(2):
                for axis in range(2):
                    ring(slot, axis, kind, True).wait_recv()
                    ring(slot, axis, kind + 2).start()

        @pl.when((j >= 2) & (j < SLOTS + 2) & taken(j - 2))
        def _():
            slot = jnp.clip(j - 2, 0, SLOTS - 1)
            for kind in range(2, 4):
                for axis in range(2):
                    ring(slot, axis, kind, True).wait_recv()

        @pl.when(j == 4)
        def _():
            swaps[9].wait_recv()
            swaps[10].wait_recv()

        pl.when(home)(lambda: own_tokens(pair))
        pl.when(visit)(lambda: mate_tokens(pair, 0))
        pass_on(2)
        pl.when(visit)(lambda: mate_tokens(pair, 1))
        pl.when((j == 6) | (j == SLOTS + 2))(lambda: feature_gram(jnp.where(j == 6, 1, PAIRS - 1)))
        pl.when(j == 2)(meet_core)
        pl.when(j == 3)(meet_mates)

    rows = lax.broadcasted_iota(jnp.int32, (LANE, LANE), 0).astype(F32)
    rows16 = lax.broadcasted_iota(jnp.int32, (16, TOK), 0).astype(F32)
    owners, values = [], ([], [])
    for pair in range(PAIRS):
        info = [slots[2 * pair + i, 0, 0:16, :].astype(F32) for i in range(2)]
        info = jnp.where(lane < PROW, info[0], info[1])
        owners.append((rows == info[TOP : TOP + 1, :]).astype(BF))
        for i in range(2):
            give_back(pair, i).wait_recv()
        for h in range(2):
            back = back_sum[pair, 0, h].astype(F32) + back_sum[pair, 1, h].astype(F32)
            values[h].append((near_sum[pair, h] + back) * xs[pair, h])
    owners = jnp.concatenate(owners, axis=1)
    sums = []
    for h in range(2):
        hi, lo = split(jnp.concatenate(values[h], axis=1))
        examples = (rows16 == marks[h, TOP : TOP + 1, :]).astype(BF)
        part = jnp.dot(examples, hi, preferred_element_type=F32) + jnp.dot(examples, lo, preferred_element_type=F32)
        sums.append(part[0:8, :])
    hi, lo = split(jnp.concatenate(sums, axis=0))
    acc[...] = nt(hi, owners) + nt(lo, owners)

    last = swap(acc.at[pl.ds(8, 8)], rbuf, 11, other)
    last.start()
    last.wait_recv()
    out_ref[...] = acc[0:EX_DEV, :] + rbuf[0:EX_DEV, :]

    last.wait_send()
    for copy in swaps:
        copy.wait_send()

    @pl.loop(0, PAIRS)
    def _(pair):
        for i in range(2):
            give_back(pair, i).wait_send()

    @pl.loop(0, SLOTS)
    def _(j):
        @pl.when(taken(j))
        def _():
            for part in range(3):
                zcopy(j, j, part).wait_send()
            for axis in range(2):
                for kind in range(4):
                    ring(j, axis, kind).wait_send()


def body(
    train_x,
    train_grad,
    train_routes,
    train_weight,
    train_example,
    probe_x,
    probe_grad,
    probe_routes,
    probe_weight,
    probe_example,
):
    hbm = pl.BlockSpec(memory_space=pl.ANY)
    vmem = pl.BlockSpec(memory_space=pltpu.VMEM)
    dma = pltpu.SemaphoreType.DMA
    return pl.pallas_call(
        kernel,
        out_shape=jax.ShapeDtypeStruct((EX_DEV, LANE), F32),
        in_specs=[hbm, hbm, vmem, vmem, vmem, hbm, hbm, vmem, vmem, vmem],
        out_specs=vmem,
        scratch_shapes=[
            pltpu.VMEM((SLOTS + 1, PANELS, PROW, LANE), BF),
            pltpu.VMEM((2, TOK, D), BF),
            pltpu.VMEM((2, TOP, TOK, KH), BF),
            pltpu.VMEM((4, TOP, TOK, KQ), BF),
            pltpu.VMEM((2, TOP, TOK, KQ), BF),
            pltpu.VMEM((TOP, PROW, KH), BF),
            pltpu.VMEM((6, TOP, TOK, LANE), F32),
            pltpu.VMEM((6, 16, LANE), F32),
            pltpu.VMEM((LANE, LANE), F32),
            pltpu.VMEM((PROW, LANE), F32),
            pltpu.VMEM((PAIRS, 2, TOK, LANE), F32),
            pltpu.VMEM((PAIRS, 2, TOK, LANE), F32),
            pltpu.VMEM((PAIRS, 2, 2, TOK, LANE), BF),
            pltpu.VMEM((PAIRS, 2, 2, TOK, LANE), BF),
            pltpu.VMEM((16, LANE), F32),
            pltpu.VMEM((8, LANE), F32),
            dma((8,)),
            dma((SLOTS, 3)),
            dma((SLOTS, 3)),
            dma((SLOTS, 2, 4)),
            dma((SLOTS, 2, 4)),
            dma((12,)),
            dma((12,)),
            dma((PAIRS, 2)),
            dma((PAIRS, 2)),
        ],
        compiler_params=pltpu.CompilerParams(
            collective_id=0, has_side_effects=True, vmem_limit_bytes=56 * 1024 * 1024
        ),
        cost_estimate=pl.CostEstimate(flops=16_000_000_000, bytes_accessed=6_000_000, transcendentals=0),
        name="ghost_scores",
    )(
        train_x,
        jnp.transpose(train_grad, (1, 0, 2)),
        train_routes.T,
        train_weight.T,
        train_example[None, :],
        probe_x,
        jnp.transpose(probe_grad, (1, 0, 2)),
        probe_routes.T,
        probe_weight.T,
        probe_example[None, :],
    )


def solution(mesh):
    in_specs = (
        P(("dp", "expert"), None),
        P(("dp", "expert"), None, None),
        P(("dp", "expert"), None),
        P(("dp", "expert"), None),
        P(("dp", "expert")),
        P("dp", None),
        P("dp", None, None),
        P("dp", None),
        P("dp", None),
        P("dp"),
    )
    out_specs = P(("dp", "expert"), None)
    return jax.shard_map(body, mesh=mesh, in_specs=in_specs, out_specs=out_specs, check_vma=False)
```

```python
import jax
import jax.numpy as jnp
from jax import lax
from jax.experimental import pallas as pl
from jax.experimental.pallas import tpu as pltpu
from jax.sharding import PartitionSpec as P

MESH = pl.DeviceIdType.MESH
BF = jnp.bfloat16
F32 = jnp.float32

LANE = 128
TOK = 128
PROW = 64
TOP = 6
D = 5120
FF = 1536
NZ = 16
NR = 4
SLOTS = 8
OWN = SLOTS
PEX_ROW = 8
EX_DEV = 4

KQ = FF // 4
KH = FF // 2

XP = D // LANE
GP = KH // LANE
X0 = 1
G0 = X0 + XP
PANELS = G0 + GP * TOP
PARTS = (10, 6)
BASES = (PANELS - NR * PARTS[0], PANELS - NR * sum(PARTS))
PAIRS = SLOTS // 2
LAG = 4


def nt(a, b):
    return lax.dot_general(a, b, (((1,), (1,)), ((), ())), preferred_element_type=F32)


def split(v):
    hi = v.astype(BF)
    return hi, (v - hi.astype(F32)).astype(BF)


def kernel(
    tx_hbm,
    tg_hbm,
    tr_ref,
    tw_ref,
    te_ref,
    px_hbm,
    pg_hbm,
    pr_ref,
    pw_ref,
    pe_ref,
    out_ref,
    slots,
    tx,
    tg,
    tgx,
    away,
    rawg,
    ids,
    marks,
    square,
    pmarks,
    xs,
    near_sum,
    far_sum,
    back_sum,
    acc,
    rbuf,
    lsem,
    zs,
    zr,
    rs,
    rr,
    es,
    er,
    qs,
    qr,
):
    z = lax.axis_index("dp")
    e = lax.axis_index("expert")
    core = e % 2
    xi = (e // 2) % NR
    yi = e // (2 * NR)
    odd = xi % 2

    def at(zz, xx, yy, cc):
        return (zz, (yy * NR + xx) * 2 + cc)

    xr, xl = (xi + 1) % NR, (xi + NR - 1) % NR
    xp, xn = xi + 1 - 2 * odd, (xi + NR - 1 + 2 * odd) % NR
    yr, yl = (yi + 1) % NR, (yi + NR - 1) % NR
    other = at(z, xi, yi, 1 - core)
    mates = (at(z, xp, yi, core), at(z, xn, yi, core))
    across = (at(z, xp, yi, 1 - core), at(z, xn, yi, 1 - core))
    sides = ((at(z, xi, yr, core), at(z, xi, yl, core)), (at(z, xr, yi, core), at(z, xl, yi, core)))
    ranks = (yi, xi)
    above = at((z + 1) % NZ, xi, yi, core)
    below = at((z + NZ - 1) % NZ, xi, yi, core)
    znext = at((z + NZ - 1 + 2 * core) % NZ, xi, yi, core)
    own = jnp.where(core == 0, OWN, 0)
    first = jnp.where(core == 0, 0, 1)

    barrier = pltpu.get_barrier_semaphore()
    greeted = (other, *mates, *across, *sides[0], above, below)
    for who in greeted:
        pl.semaphore_signal(barrier, inc=1, device_id=who, device_id_type=MESH)

    def quarter(i):
        return pl.ds(pl.multiple_of(i * KQ, LANE), KQ)

    mine = (quarter(odd), quarter(3 - odd))
    theirs = (quarter(1 - odd), quarter(2 + odd))
    parts = (pl.ds(0, KQ), pl.ds(KQ, KQ))
    probe_load = [
        pltpu.make_async_copy(pg_hbm.at[:, :, mine[i]], rawg.at[:, :, parts[i]], lsem.at[i]) for i in range(2)
    ]
    for copy in probe_load:
        copy.start()

    @pl.loop(0, XP)
    def _(c):
        cols = pl.ds(pl.multiple_of(c * LANE, LANE), LANE)
        pltpu.make_async_copy(px_hbm.at[:, cols], slots.at[own, X0 + c], lsem.at[2]).start()

    away_load = [pltpu.make_async_copy(tg_hbm.at[:, :, theirs[i]], away.at[i], lsem.at[3 + i]) for i in range(2)]
    grad_load = [
        pltpu.make_async_copy(tg_hbm.at[:, :, mine[i]], tg.at[0, :, :, parts[i]], lsem.at[5 + i]) for i in range(2)
    ]
    for copy in away_load + grad_load:
        copy.start()
    x_load = pltpu.make_async_copy(tx_hbm, tx.at[0], lsem.at[7])
    x_load.start()

    lane = lax.broadcasted_iota(jnp.int32, (1, LANE), 1)
    square[...] = jnp.zeros_like(square)
    square[0:TOP, 0:PROW] = pr_ref[...].astype(F32)
    square[TOP : TOP + 1, 0:PROW] = pe_ref[...].astype(F32)
    square[8 : 8 + TOP, 0:PROW] = pw_ref[...]
    near = square[0:8, :]
    both = near + pltpu.roll(near, PROW, 1)
    pmarks[...] = jnp.zeros_like(pmarks)
    pmarks[0:TOP, :] = both[0:TOP, :]
    pmarks[TOP : TOP + 1, :] = both[TOP : TOP + 1, :] + (z * PEX_ROW).astype(F32)
    slots[own, 0] = pmarks[...].astype(BF)

    turned = jnp.transpose(square[...])
    for copy in probe_load:
        copy.wait()
    for q in range(TOP):
        scale = jnp.broadcast_to(turned[0:PROW, 8 + q : 9 + q], (PROW, LANE))
        for k in range(GP):
            block = rawg[q, :, k * LANE : (k + 1) * LANE].astype(F32)
            slots[own, G0 + k * TOP + q] = (block * scale).astype(BF)
    pltpu.make_async_copy(slots.at[own, pl.ds(X0, XP)], slots.at[own, pl.ds(X0, XP)], lsem.at[2]).wait()

    def remote(src, dst, send, recv, who):
        return pltpu.make_async_remote_copy(
            src_ref=src, dst_ref=dst, send_sem=send, recv_sem=recv, device_id=who, device_id_type=MESH
        )

    def share(slot, axis, who, begin, count):
        return slots.at[slot, pl.ds(BASES[axis] + PARTS[axis] * who + begin, count)]

    def zcopy(src, dst, part):
        if part < 2:
            pick = lambda slot: share(slot, part, ranks[part], 0, PARTS[part])
        else:
            pick = lambda slot: slots.at[slot, pl.ds(0, BASES[1])]
        return remote(pick(src), pick(dst), zs.at[dst, part], zr.at[dst, part], znext)

    def ring(slot, axis, kind, landing=False):
        size = PARTS[axis]
        who = (0, 0, NR - 1, 1)[kind] + ((NR - 1, 1)[kind % 2] if landing else 0)
        begin, count = ((0, size), (0, size), (0, size // 2), (size // 2, size - size // 2))[kind]
        region = share(slot, axis, (ranks[axis] + who) % NR, begin, count)
        return remote(region, region, rs.at[slot, axis, kind], rr.at[slot, axis, kind], sides[axis][kind % 2])

    pl.semaphore_wait(barrier, len(greeted))
    for part in range(3):
        zcopy(own, first, part).start()

    marks[0] = jnp.zeros((16, LANE), F32)
    marks[0, 0:TOP, :] = tr_ref[...].astype(F32)
    marks[0, TOP : TOP + 1, :] = te_ref[...].astype(F32)
    square[...] = jnp.zeros_like(square)
    square[0:TOP, :] = tr_ref[...].astype(F32)
    square[8 : 8 + TOP, :] = tw_ref[...]
    turned = jnp.transpose(square[...])

    def scale_train(ref, panels):
        for r in range(TOP):
            scale = jnp.broadcast_to(turned[:, 8 + r : 9 + r], (TOK, LANE))

            @pl.loop(0, panels)
            def _(k):
                cols = pl.ds(pl.multiple_of(k * LANE, LANE), LANE)
                ref[r, :, cols] = (ref[r, :, cols].astype(F32) * scale).astype(BF)

    def spread(group):
        square[0:16, :] = marks[group]
        columns = jnp.transpose(square[...])
        for r in range(TOP):
            ids[group, r] = jnp.broadcast_to(columns[:, r : r + 1], (TOK, LANE))

    def swap(src, dst, which, who):
        return remote(src, dst, es.at[which], er.at[which], who)

    swaps = (
        swap(marks.at[0], marks.at[1], 0, other),
        swap(marks.at[0], marks.at[2], 1, mates[0]),
        swap(marks.at[0], marks.at[3], 2, across[0]),
        swap(marks.at[0], marks.at[4], 3, mates[1]),
        swap(marks.at[0], marks.at[5], 4, across[1]),
        swap(away.at[0], tgx.at[0], 5, mates[0]),
        swap(away.at[1], tgx.at[2], 6, mates[1]),
        swap(tx.at[0], tx.at[1], 7, other),
        swap(tg.at[0], tg.at[1], 8, other),
        swap(tgx.at[0], tgx.at[1], 9, other),
        swap(tgx.at[2], tgx.at[3], 10, other),
    )
    for i in range(2):
        away_load[i].wait()
        scale_train(away.at[i], KQ // LANE)
        swaps[5 + i].start()
    for which in range(5):
        swaps[which].start()
    x_load.wait()
    swaps[7].start()
    for copy in grad_load:
        copy.wait()
    scale_train(tg.at[0], GP)
    swaps[8].start()
    spread(0)

    def meet_core():
        swaps[0].wait_recv()
        spread(1)
        swaps[7].wait_recv()
        swaps[8].wait_recv()

    def meet_mates():
        for i in range(2):
            swaps[5 + i].wait_recv()
            swaps[9 + i].start()
        for group in range(2, 6):
            swaps[group - 1].wait_recv()
            spread(group)

    def feature_gram(pair):
        px = [jnp.concatenate([slots[2 * pair - 2 + i, X0 + c] for c in range(XP)], axis=1) for i in range(4)]
        gram = nt(tx[...].reshape(2 * TOK, D), jnp.concatenate(px, axis=0))
        for i in range(2):
            for h in range(2):
                xs[pair - 1 + i, h] = gram[h * TOK : (h + 1) * TOK, i * LANE : (i + 1) * LANE]

    def route_gram(pair, lhs, group, panels):
        info = [slots[2 * pair + i, 0, 0:16, :].astype(F32) for i in range(2)]
        info = jnp.where(lane < PROW, info[0], info[1])
        pg = jnp.concatenate(
            [
                jnp.concatenate(
                    [slots[2 * pair + i, G0 + k * TOP + q] for q in range(TOP) for i in range(2)], axis=0
                )
                for k in panels
            ],
            axis=1,
        )
        gram = nt(lhs.reshape(TOP * TOK, len(panels) * LANE), pg)
        total = jnp.zeros((TOK, LANE), F32)
        for r in range(TOP):
            who = ids[group, r]
            for q in range(TOP):
                part = gram[r * TOK : (r + 1) * TOK, q * LANE : (q + 1) * LANE]
                total = total + jnp.where(who == info[q : q + 1, :], part, 0.0)
        return total

    def give_back(pair, i):
        return remote(far_sum.at[pair, i], back_sum.at[pair, i], qs.at[pair, i], qr.at[pair, i], mates[i])

    def own_tokens(pair):
        for h in range(2):
            near_sum[pair, h] = route_gram(pair, tg[h], h, range(GP))

    def mate_tokens(pair, i):
        for h in range(2):
            panels = range(i * GP // 2, (i + 1) * GP // 2)
            far_sum[pair, i, h] = route_gram(pair, tgx[2 * i + h], 2 + 2 * i + h, panels).astype(BF)
        give_back(pair, i).start()

    def taken(j):
        return (core == 0) | (j >= 1)

    @pl.loop(0, SLOTS + LAG)
    def _(j):
        fresh = (j < SLOTS) & taken(j)
        ready = j >= LAG
        since = jnp.maximum(j - LAG, 0)
        pair = since // 2
        at_home = (since % 2 == 0) != (pair == PAIRS - 1)

        def pass_on(part):
            @pl.when(fresh)
            def _():
                zcopy(j, j, part).wait_recv()

                @pl.when(j < SLOTS - 1)
                def _():
                    zcopy(j, jnp.minimum(j + 1, SLOTS - 1), part).start()

                if part < 2:
                    ring(j, part, 0).start()
                    ring(j, part, 1).start()

        def hop():
            slot = jnp.clip(j - 1, 0, SLOTS - 1)
            for kind in range(2):
                for axis in range(2):
                    ring(slot, axis, kind, True).wait_recv()
                    ring(slot, axis, kind + 2).start()

        pass_on(0)
        pl.when(j == SLOTS)(hop)

        @pl.when(j == LAG + 1)
        def _():
            swaps[9].wait_recv()
            swaps[10].wait_recv()

        pl.when(ready & at_home & (pair % 2 == 1))(lambda: feature_gram(jnp.maximum(pair, 1)))
        pl.when(ready & ~at_home)(lambda: mate_tokens(pair, 0))
        pass_on(1)
        pl.when(ready & at_home)(lambda: own_tokens(pair))
        pl.when(ready & ~at_home)(lambda: mate_tokens(pair, 1))
        pass_on(2)
        pl.when(j == LAG - 1)(meet_core)

        pl.when((j >= 1) & (j < SLOTS) & taken(j - 1))(hop)

        pl.when(j == LAG)(meet_mates)

        @pl.when((j >= 2) & (j < SLOTS + 2) & taken(j - 2))
        def _():
            slot = jnp.maximum(j - 2, 0)
            for kind in range(2, 4):
                for axis in range(2):
                    ring(slot, axis, kind, True).wait_recv()

    rows = lax.broadcasted_iota(jnp.int32, (LANE, LANE), 0).astype(F32)
    rows16 = lax.broadcasted_iota(jnp.int32, (16, TOK), 0).astype(F32)
    owners, values = [], ([], [])
    for pair in range(PAIRS):
        info = [slots[2 * pair + i, 0, 0:16, :].astype(F32) for i in range(2)]
        info = jnp.where(lane < PROW, info[0], info[1])
        owners.append((rows == info[TOP : TOP + 1, :]).astype(BF))
        for i in range(2):
            give_back(pair, i).wait_recv()
        for h in range(2):
            back = back_sum[pair, 0, h].astype(F32) + back_sum[pair, 1, h].astype(F32)
            values[h].append((near_sum[pair, h] + back) * xs[pair, h])
    owners = jnp.concatenate(owners, axis=1)
    sums = []
    for h in range(2):
        hi, lo = split(jnp.concatenate(values[h], axis=1))
        examples = (rows16 == marks[h, TOP : TOP + 1, :]).astype(BF)
        part = jnp.dot(examples, hi, preferred_element_type=F32) + jnp.dot(examples, lo, preferred_element_type=F32)
        sums.append(part[0:8, :])
    hi, lo = split(jnp.concatenate(sums, axis=0))
    acc[...] = nt(hi, owners) + nt(lo, owners)

    last = swap(acc.at[pl.ds(8, 8)], rbuf, 11, other)
    last.start()
    last.wait_recv()
    out_ref[...] = acc[0:EX_DEV, :] + rbuf[0:EX_DEV, :]

    last.wait_send()
    for copy in swaps:
        copy.wait_send()

    @pl.loop(0, PAIRS)
    def _(pair):
        for i in range(2):
            give_back(pair, i).wait_send()

    @pl.loop(0, SLOTS)
    def _(j):
        @pl.when(taken(j))
        def _():
            for part in range(3):
                zcopy(j, j, part).wait_send()
            for axis in range(2):
                for kind in range(4):
                    ring(j, axis, kind).wait_send()


def body(
    train_x,
    train_grad,
    train_routes,
    train_weight,
    train_example,
    probe_x,
    probe_grad,
    probe_routes,
    probe_weight,
    probe_example,
):
    hbm = pl.BlockSpec(memory_space=pl.ANY)
    vmem = pl.BlockSpec(memory_space=pltpu.VMEM)
    dma = pltpu.SemaphoreType.DMA
    return pl.pallas_call(
        kernel,
        out_shape=jax.ShapeDtypeStruct((EX_DEV, LANE), F32),
        in_specs=[hbm, hbm, vmem, vmem, vmem, hbm, hbm, vmem, vmem, vmem],
        out_specs=vmem,
        scratch_shapes=[
            pltpu.VMEM((SLOTS + 1, PANELS, PROW, LANE), BF),
            pltpu.VMEM((2, TOK, D), BF),
            pltpu.VMEM((2, TOP, TOK, KH), BF),
            pltpu.VMEM((4, TOP, TOK, KQ), BF),
            pltpu.VMEM((2, TOP, TOK, KQ), BF),
            pltpu.VMEM((TOP, PROW, KH), BF),
            pltpu.VMEM((6, TOP, TOK, LANE), F32),
            pltpu.VMEM((6, 16, LANE), F32),
            pltpu.VMEM((LANE, LANE), F32),
            pltpu.VMEM((PROW, LANE), F32),
            pltpu.VMEM((PAIRS, 2, TOK, LANE), F32),
            pltpu.VMEM((PAIRS, 2, TOK, LANE), F32),
            pltpu.VMEM((PAIRS, 2, 2, TOK, LANE), BF),
            pltpu.VMEM((PAIRS, 2, 2, TOK, LANE), BF),
            pltpu.VMEM((16, LANE), F32),
            pltpu.VMEM((8, LANE), F32),
            dma((8,)),
            dma((SLOTS, 3)),
            dma((SLOTS, 3)),
            dma((SLOTS, 2, 4)),
            dma((SLOTS, 2, 4)),
            dma((12,)),
            dma((12,)),
            dma((PAIRS, 2)),
            dma((PAIRS, 2)),
        ],
        compiler_params=pltpu.CompilerParams(
            collective_id=0, has_side_effects=True, vmem_limit_bytes=56 * 1024 * 1024
        ),
        cost_estimate=pl.CostEstimate(flops=16_000_000_000, bytes_accessed=6_000_000, transcendentals=0),
        name="ghost_scores",
    )(
        train_x,
        jnp.transpose(train_grad, (1, 0, 2)),
        train_routes.T,
        train_weight.T,
        train_example[None, :],
        probe_x,
        jnp.transpose(probe_grad, (1, 0, 2)),
        probe_routes.T,
        probe_weight.T,
        probe_example[None, :],
    )


def solution(mesh):
    in_specs = (
        P(("dp", "expert"), None),
        P(("dp", "expert"), None, None),
        P(("dp", "expert"), None),
        P(("dp", "expert"), None),
        P(("dp", "expert")),
        P("dp", None),
        P("dp", None, None),
        P("dp", None),
        P("dp", None),
        P("dp"),
    )
    out_specs = P(("dp", "expert"), None)
    return jax.shard_map(body, mesh=mesh, in_specs=in_specs, out_specs=out_specs, check_vma=False)
```

```python
import jax
import jax.numpy as jnp
from jax import lax
from jax.experimental import pallas as pl
from jax.experimental.pallas import tpu as pltpu
from jax.sharding import PartitionSpec as P

MESH = pl.DeviceIdType.MESH
BF = jnp.bfloat16
F32 = jnp.float32

LANE = 128
TOK = 128
PROW = 64
TOP = 6
D = 5120
FF = 1536
NZ = 16
NR = 4
SLOTS = 8
OWN = SLOTS
PEX_ROW = 8
EX_DEV = 4

KQ = FF // 4
KH = FF // 2

XP = D // LANE
GP = KH // LANE
X0 = 1
G0 = X0 + XP
PANELS = G0 + GP * TOP
PARTS = (11, 7)
BASES = (PANELS - NR * PARTS[0], PANELS - NR * sum(PARTS))
PAIRS = SLOTS // 2
LAG = 4


def nt(a, b):
    return lax.dot_general(a, b, (((1,), (1,)), ((), ())), preferred_element_type=F32)


def split(v):
    hi = v.astype(BF)
    return hi, (v - hi.astype(F32)).astype(BF)


def kernel(
    tx_hbm,
    tg_hbm,
    tr_ref,
    tw_ref,
    te_ref,
    px_hbm,
    pg_hbm,
    pr_ref,
    pw_ref,
    pe_ref,
    out_ref,
    slots,
    tx,
    tg,
    tgx,
    away,
    rawg,
    ids,
    marks,
    square,
    pmarks,
    xs,
    near_sum,
    far_sum,
    back_sum,
    acc,
    rbuf,
    lsem,
    zs,
    zr,
    rs,
    rr,
    es,
    er,
    qs,
    qr,
):
    z = lax.axis_index("dp")
    e = lax.axis_index("expert")
    core = e % 2
    xi = (e // 2) % NR
    yi = e // (2 * NR)
    odd = xi % 2

    def at(zz, xx, yy, cc):
        return (zz, (yy * NR + xx) * 2 + cc)

    xr, xl = (xi + 1) % NR, (xi + NR - 1) % NR
    xp, xn = xi + 1 - 2 * odd, (xi + NR - 1 + 2 * odd) % NR
    yr, yl = (yi + 1) % NR, (yi + NR - 1) % NR
    other = at(z, xi, yi, 1 - core)
    mates = (at(z, xp, yi, core), at(z, xn, yi, core))
    across = (at(z, xp, yi, 1 - core), at(z, xn, yi, 1 - core))
    sides = ((at(z, xi, yr, core), at(z, xi, yl, core)), (at(z, xr, yi, core), at(z, xl, yi, core)))
    ranks = (yi, xi)
    above = at((z + 1) % NZ, xi, yi, core)
    below = at((z + NZ - 1) % NZ, xi, yi, core)
    znext = at((z + NZ - 1 + 2 * core) % NZ, xi, yi, core)
    own = jnp.where(core == 0, OWN, 0)
    first = jnp.where(core == 0, 0, 1)

    barrier = pltpu.get_barrier_semaphore()
    greeted = (other, *mates, *across, *sides[0], above, below)
    for who in greeted:
        pl.semaphore_signal(barrier, inc=1, device_id=who, device_id_type=MESH)

    def quarter(i):
        return pl.ds(pl.multiple_of(i * KQ, LANE), KQ)

    mine = (quarter(odd), quarter(3 - odd))
    theirs = (quarter(1 - odd), quarter(2 + odd))
    parts = (pl.ds(0, KQ), pl.ds(KQ, KQ))
    probe_load = [
        pltpu.make_async_copy(pg_hbm.at[:, :, mine[i]], rawg.at[:, :, parts[i]], lsem.at[i]) for i in range(2)
    ]
    for copy in probe_load:
        copy.start()

    @pl.loop(0, XP)
    def _(c):
        cols = pl.ds(pl.multiple_of(c * LANE, LANE), LANE)
        pltpu.make_async_copy(px_hbm.at[:, cols], slots.at[own, X0 + c], lsem.at[2]).start()

    away_load = [pltpu.make_async_copy(tg_hbm.at[:, :, theirs[i]], away.at[i], lsem.at[3 + i]) for i in range(2)]
    grad_load = [
        pltpu.make_async_copy(tg_hbm.at[:, :, mine[i]], tg.at[0, :, :, parts[i]], lsem.at[5 + i]) for i in range(2)
    ]
    for copy in away_load + grad_load:
        copy.start()
    x_load = pltpu.make_async_copy(tx_hbm, tx.at[0], lsem.at[7])
    x_load.start()

    lane = lax.broadcasted_iota(jnp.int32, (1, LANE), 1)
    square[...] = jnp.zeros_like(square)
    square[0:TOP, 0:PROW] = pr_ref[...].astype(F32)
    square[TOP : TOP + 1, 0:PROW] = pe_ref[...].astype(F32)
    square[8 : 8 + TOP, 0:PROW] = pw_ref[...]
    near = square[0:8, :]
    both = near + pltpu.roll(near, PROW, 1)
    pmarks[...] = jnp.zeros_like(pmarks)
    pmarks[0:TOP, :] = both[0:TOP, :]
    pmarks[TOP : TOP + 1, :] = both[TOP : TOP + 1, :] + (z * PEX_ROW).astype(F32)
    slots[own, 0] = pmarks[...].astype(BF)

    turned = jnp.transpose(square[...])
    for copy in probe_load:
        copy.wait()
    for q in range(TOP):
        scale = jnp.broadcast_to(turned[0:PROW, 8 + q : 9 + q], (PROW, LANE))
        for k in range(GP):
            block = rawg[q, :, k * LANE : (k + 1) * LANE].astype(F32)
            slots[own, G0 + k * TOP + q] = (block * scale).astype(BF)
    pltpu.make_async_copy(slots.at[own, pl.ds(X0, XP)], slots.at[own, pl.ds(X0, XP)], lsem.at[2]).wait()

    def remote(src, dst, send, recv, who):
        return pltpu.make_async_remote_copy(
            src_ref=src, dst_ref=dst, send_sem=send, recv_sem=recv, device_id=who, device_id_type=MESH
        )

    def share(slot, axis, who, begin, count):
        return slots.at[slot, pl.ds(BASES[axis] + PARTS[axis] * who + begin, count)]

    def zcopy(src, dst, part):
        if part < 2:
            pick = lambda slot: share(slot, part, ranks[part], 0, PARTS[part])
        else:
            pick = lambda slot: slots.at[slot, pl.ds(0, BASES[1])]
        return remote(pick(src), pick(dst), zs.at[dst, part], zr.at[dst, part], znext)

    def ring(slot, axis, kind, landing=False):
        size = PARTS[axis]
        who = (0, 0, NR - 1, 1)[kind] + ((NR - 1, 1)[kind % 2] if landing else 0)
        begin, count = ((0, size), (0, size), (0, size // 2), (size // 2, size - size // 2))[kind]
        region = share(slot, axis, (ranks[axis] + who) % NR, begin, count)
        return remote(region, region, rs.at[slot, axis, kind], rr.at[slot, axis, kind], sides[axis][kind % 2])

    pl.semaphore_wait(barrier, len(greeted))
    for part in range(3):
        zcopy(own, first, part).start()

    marks[0] = jnp.zeros((16, LANE), F32)
    marks[0, 0:TOP, :] = tr_ref[...].astype(F32)
    marks[0, TOP : TOP + 1, :] = te_ref[...].astype(F32)
    square[...] = jnp.zeros_like(square)
    square[0:TOP, :] = tr_ref[...].astype(F32)
    square[8 : 8 + TOP, :] = tw_ref[...]
    turned = jnp.transpose(square[...])

    def scale_train(ref, panels):
        for r in range(TOP):
            scale = jnp.broadcast_to(turned[:, 8 + r : 9 + r], (TOK, LANE))

            @pl.loop(0, panels)
            def _(k):
                cols = pl.ds(pl.multiple_of(k * LANE, LANE), LANE)
                ref[r, :, cols] = (ref[r, :, cols].astype(F32) * scale).astype(BF)

    def spread(group):
        square[0:16, :] = marks[group]
        columns = jnp.transpose(square[...])
        for r in range(TOP):
            ids[group, r] = jnp.broadcast_to(columns[:, r : r + 1], (TOK, LANE))

    def swap(src, dst, which, who):
        return remote(src, dst, es.at[which], er.at[which], who)

    swaps = (
        swap(marks.at[0], marks.at[1], 0, other),
        swap(marks.at[0], marks.at[2], 1, mates[0]),
        swap(marks.at[0], marks.at[3], 2, across[0]),
        swap(marks.at[0], marks.at[4], 3, mates[1]),
        swap(marks.at[0], marks.at[5], 4, across[1]),
        swap(away.at[0], tgx.at[0], 5, mates[0]),
        swap(away.at[1], tgx.at[2], 6, mates[1]),
        swap(tx.at[0], tx.at[1], 7, other),
        swap(tg.at[0], tg.at[1], 8, other),
        swap(tgx.at[0], tgx.at[1], 9, other),
        swap(tgx.at[2], tgx.at[3], 10, other),
    )
    for i in range(2):
        away_load[i].wait()
        scale_train(away.at[i], KQ // LANE)
        swaps[5 + i].start()
    for which in range(5):
        swaps[which].start()
    x_load.wait()
    swaps[7].start()
    for copy in grad_load:
        copy.wait()
    scale_train(tg.at[0], GP)
    swaps[8].start()
    spread(0)

    def meet_core():
        swaps[0].wait_recv()
        spread(1)
        swaps[7].wait_recv()
        swaps[8].wait_recv()

    def meet_mates():
        for i in range(2):
            swaps[5 + i].wait_recv()
            swaps[9 + i].start()
        for group in range(2, 6):
            swaps[group - 1].wait_recv()
            spread(group)

    def feature_gram(pair):
        px = [jnp.concatenate([slots[2 * pair - 2 + i, X0 + c] for c in range(XP)], axis=1) for i in range(4)]
        gram = nt(tx[...].reshape(2 * TOK, D), jnp.concatenate(px, axis=0))
        for i in range(2):
            for h in range(2):
                xs[pair - 1 + i, h] = gram[h * TOK : (h + 1) * TOK, i * LANE : (i + 1) * LANE]

    def route_gram(pair, lhs, group, panels):
        info = [slots[2 * pair + i, 0, 0:16, :].astype(F32) for i in range(2)]
        info = jnp.where(lane < PROW, info[0], info[1])
        pg = jnp.concatenate(
            [
                jnp.concatenate(
                    [slots[2 * pair + i, G0 + k * TOP + q] for q in range(TOP) for i in range(2)], axis=0
                )
                for k in panels
            ],
            axis=1,
        )
        gram = nt(lhs.reshape(TOP * TOK, len(panels) * LANE), pg)
        total = jnp.zeros((TOK, LANE), F32)
        for r in range(TOP):
            who = ids[group, r]
            for q in range(TOP):
                part = gram[r * TOK : (r + 1) * TOK, q * LANE : (q + 1) * LANE]
                total = total + jnp.where(who == info[q : q + 1, :], part, 0.0)
        return total

    def give_back(pair, i):
        return remote(far_sum.at[pair, i], back_sum.at[pair, i], qs.at[pair, i], qr.at[pair, i], mates[i])

    def own_tokens(pair):
        for h in range(2):
            near_sum[pair, h] = route_gram(pair, tg[h], h, range(GP))

    def mate_tokens(pair, i):
        for h in range(2):
            panels = range(i * GP // 2, (i + 1) * GP // 2)
            far_sum[pair, i, h] = route_gram(pair, tgx[2 * i + h], 2 + 2 * i + h, panels).astype(BF)
        give_back(pair, i).start()

    def taken(j):
        return (core == 0) | (j >= 1)

    @pl.loop(0, SLOTS + LAG)
    def _(j):
        fresh = (j < SLOTS) & taken(j)
        ready = j >= LAG
        since = jnp.maximum(j - LAG, 0)
        pair = since // 2
        at_home = (since % 2 == 0) != (pair == PAIRS - 1)

        def pass_on(part):
            @pl.when(fresh)
            def _():
                zcopy(j, j, part).wait_recv()

                @pl.when(j < SLOTS - 1)
                def _():
                    zcopy(j, jnp.minimum(j + 1, SLOTS - 1), part).start()

                if part < 2:
                    ring(j, part, 0).start()
                    ring(j, part, 1).start()

        def hop():
            slot = jnp.clip(j - 1, 0, SLOTS - 1)
            for kind in range(2):
                for axis in range(2):
                    ring(slot, axis, kind, True).wait_recv()
                    ring(slot, axis, kind + 2).start()

        pass_on(0)
        pl.when(j == SLOTS)(hop)

        @pl.when(j == LAG + 1)
        def _():
            swaps[9].wait_recv()
            swaps[10].wait_recv()

        pl.when(ready & at_home & (pair % 2 == 1))(lambda: feature_gram(jnp.maximum(pair, 1)))
        pl.when(ready & ~at_home)(lambda: mate_tokens(pair, 0))
        pass_on(1)
        pl.when(ready & at_home)(lambda: own_tokens(pair))
        pl.when(ready & ~at_home)(lambda: mate_tokens(pair, 1))
        pass_on(2)
        pl.when(j == LAG - 1)(meet_core)

        pl.when((j >= 1) & (j < SLOTS) & taken(j - 1))(hop)

        pl.when(j == LAG)(meet_mates)

        @pl.when((j >= 2) & (j < SLOTS + 2) & taken(j - 2))
        def _():
            slot = jnp.maximum(j - 2, 0)
            for kind in range(2, 4):
                for axis in range(2):
                    ring(slot, axis, kind, True).wait_recv()

    rows = lax.broadcasted_iota(jnp.int32, (LANE, LANE), 0).astype(F32)
    rows16 = lax.broadcasted_iota(jnp.int32, (16, TOK), 0).astype(F32)
    owners, values = [], ([], [])
    for pair in range(PAIRS):
        info = [slots[2 * pair + i, 0, 0:16, :].astype(F32) for i in range(2)]
        info = jnp.where(lane < PROW, info[0], info[1])
        owners.append((rows == info[TOP : TOP + 1, :]).astype(BF))
        for i in range(2):
            give_back(pair, i).wait_recv()
        for h in range(2):
            back = back_sum[pair, 0, h].astype(F32) + back_sum[pair, 1, h].astype(F32)
            values[h].append((near_sum[pair, h] + back) * xs[pair, h])
    owners = jnp.concatenate(owners, axis=1)
    sums = []
    for h in range(2):
        hi, lo = split(jnp.concatenate(values[h], axis=1))
        examples = (rows16 == marks[h, TOP : TOP + 1, :]).astype(BF)
        part = jnp.dot(examples, hi, preferred_element_type=F32) + jnp.dot(examples, lo, preferred_element_type=F32)
        sums.append(part[0:8, :])
    hi, lo = split(jnp.concatenate(sums, axis=0))
    acc[...] = nt(hi, owners) + nt(lo, owners)

    last = swap(acc.at[pl.ds(8, 8)], rbuf, 11, other)
    last.start()
    last.wait_recv()
    out_ref[...] = acc[0:EX_DEV, :] + rbuf[0:EX_DEV, :]

    last.wait_send()
    for copy in swaps:
        copy.wait_send()

    @pl.loop(0, PAIRS)
    def _(pair):
        for i in range(2):
            give_back(pair, i).wait_send()

    @pl.loop(0, SLOTS)
    def _(j):
        @pl.when(taken(j))
        def _():
            for part in range(3):
                zcopy(j, j, part).wait_send()
            for axis in range(2):
                for kind in range(4):
                    ring(j, axis, kind).wait_send()


def body(
    train_x,
    train_grad,
    train_routes,
    train_weight,
    train_example,
    probe_x,
    probe_grad,
    probe_routes,
    probe_weight,
    probe_example,
):
    hbm = pl.BlockSpec(memory_space=pl.ANY)
    vmem = pl.BlockSpec(memory_space=pltpu.VMEM)
    dma = pltpu.SemaphoreType.DMA
    return pl.pallas_call(
        kernel,
        out_shape=jax.ShapeDtypeStruct((EX_DEV, LANE), F32),
        in_specs=[hbm, hbm, vmem, vmem, vmem, hbm, hbm, vmem, vmem, vmem],
        out_specs=vmem,
        scratch_shapes=[
            pltpu.VMEM((SLOTS + 1, PANELS, PROW, LANE), BF),
            pltpu.VMEM((2, TOK, D), BF),
            pltpu.VMEM((2, TOP, TOK, KH), BF),
            pltpu.VMEM((4, TOP, TOK, KQ), BF),
            pltpu.VMEM((2, TOP, TOK, KQ), BF),
            pltpu.VMEM((TOP, PROW, KH), BF),
            pltpu.VMEM((6, TOP, TOK, LANE), F32),
            pltpu.VMEM((6, 16, LANE), F32),
            pltpu.VMEM((LANE, LANE), F32),
            pltpu.VMEM((PROW, LANE), F32),
            pltpu.VMEM((PAIRS, 2, TOK, LANE), F32),
            pltpu.VMEM((PAIRS, 2, TOK, LANE), F32),
            pltpu.VMEM((PAIRS, 2, 2, TOK, LANE), BF),
            pltpu.VMEM((PAIRS, 2, 2, TOK, LANE), BF),
            pltpu.VMEM((16, LANE), F32),
            pltpu.VMEM((8, LANE), F32),
            dma((8,)),
            dma((SLOTS, 3)),
            dma((SLOTS, 3)),
            dma((SLOTS, 2, 4)),
            dma((SLOTS, 2, 4)),
            dma((12,)),
            dma((12,)),
            dma((PAIRS, 2)),
            dma((PAIRS, 2)),
        ],
        compiler_params=pltpu.CompilerParams(
            collective_id=0, has_side_effects=True, vmem_limit_bytes=56 * 1024 * 1024
        ),
        cost_estimate=pl.CostEstimate(flops=16_000_000_000, bytes_accessed=6_000_000, transcendentals=0),
        name="ghost_scores",
    )(
        train_x,
        jnp.transpose(train_grad, (1, 0, 2)),
        train_routes.T,
        train_weight.T,
        train_example[None, :],
        probe_x,
        jnp.transpose(probe_grad, (1, 0, 2)),
        probe_routes.T,
        probe_weight.T,
        probe_example[None, :],
    )


def solution(mesh):
    in_specs = (
        P(("dp", "expert"), None),
        P(("dp", "expert"), None, None),
        P(("dp", "expert"), None),
        P(("dp", "expert"), None),
        P(("dp", "expert")),
        P("dp", None),
        P("dp", None, None),
        P("dp", None),
        P("dp", None),
        P("dp"),
    )
    out_specs = P(("dp", "expert"), None)
    return jax.shard_map(body, mesh=mesh, in_specs=in_specs, out_specs=out_specs, check_vma=False)
```
